512 devices in a mesh: gx: 16 (over z), gy: 32 (over x, y, core).
Axes of the slice: x: 4, y: 4, z: 16, core: 2. Of those that a mesh axis runs over, the one named last changes fastest.
Arguments:
- particles: bfloat16 [32768, 4096], P(('gx', 'gy')), may hold values from -6 to 6
- references: bfloat16 [16, 12, 4096], P('gx'), may hold values from -1 to 1
- slot_class: int32 [16], replicated, may hold values from 0 to 15, each once
- log_prior: float32 [16], replicated, may hold values from -2 to 2
- shift_offsets: int32 [8, 2], replicated, may hold values from -8 to 8
- group_ids: int32 [32768], P(('gx', 'gy')), may hold values from 0 to 127
- ctf_table: float32 [128, 2048], replicated, may hold values from -1 to 1
- noise_power: float32 [2048], replicated, may hold values from 0.5 to 2
Outputs:
- class_sums: float32 [16, 12, 4096], P('gx')
- ctf_power: float32 [16, 2048], P('gx')
- log_evidence: float32 [], replicated
The draws below stay inside these ranges and needn't reach their ends.
Inputs may be any that keep to these rules, and one draw needn't show every extreme that they name: `slot_class`: each class id stands at exactly one slot.
All inputs are finite; a program needn't handle non-finite values.
Results may differ from the reference program's by a relative error of at most 0.006.
Values may be sent and summed in bfloat16 or wider, within the bound.
A program may use at most 64 MiB of HBM per device.

```python
import math
import jax
import jax.numpy as jnp
from jax import lax

L = 64
R = 12
NS = 8
G = 128
PART_DEV = 64
HALF = 2048
FR = 4096
CLASSES = 16
PARTICLES = 32768
N_GX = 16
N_GY = 32


def plant(values, own_key, smallest, largest):
    longest = values.shape.index(max(values.shape))
    spots = []
    for shift in (0, 1):
        where = [jax.random.randint(jax.random.fold_in(own_key, axis), (), 0, length) for axis, length in enumerate(values.shape)]
        where[longest] = (where[longest] + shift) % values.shape[longest]
        spots.append(tuple(where))
    return values.at[spots[0]].set(smallest).at[spots[1]].set(largest)


def steps_of(key, shape, cuts, smallest, high):
    factor_of = 1.0
    for position, shards_of in cuts:
        draws = jax.random.uniform(jax.random.fold_in(jax.random.fold_in(key, 6), position), (shards_of,), jnp.float32, smallest / len(cuts), high / len(cuts))
        factor_of = factor_of * jnp.repeat(jnp.exp(draws), shape[position] // shards_of).reshape((-1,) + (1,) * (len(shape) - 1 - position))
    return factor_of


def gaussian(rng, extent, deviation, most, shards=(), held_as=jnp.bfloat16):
    array = deviation * jax.random.normal(rng, extent, jnp.float32)
    if shards:
        array = array * steps_of(rng, extent, shards, -0.22, 0.18)
    return jnp.clip(array, -most, most).astype(held_as)


def setup_inputs(seed: int = 0) -> dict:
    arg_keys = jax.random.split(jax.random.key(seed), 9)
    return {
        "particles": gaussian(arg_keys[0], (PARTICLES, L * L), 1.0, 6.0, ((0, 512),)),
        "references": gaussian(arg_keys[1], (CLASSES, R, FR), 0.07, 1.0, ((0, 16),)),
        "slot_class": jax.random.permutation(arg_keys[2], CLASSES).astype(jnp.int32),
        "log_prior": jnp.clip(jax.random.uniform(arg_keys[3], (CLASSES,), jnp.float32, -2.0, 2.0), -2.0, 2.0),
        "shift_offsets": plant(jax.random.randint(arg_keys[4], (NS, 2), -8, 9), jax.random.fold_in(arg_keys[4], 1), -8, 8).astype(jnp.int32),
        "group_ids": plant(jax.random.randint(arg_keys[5], (PARTICLES,), 0, G), jax.random.fold_in(arg_keys[5], 1), 0, G - 1).astype(jnp.int32),
        "ctf_table": jnp.clip(jax.random.uniform(arg_keys[6], (G, HALF), jnp.float32, -1.0, 1.0), -1.0, 1.0),
        "noise_power": jnp.clip(jnp.exp(jax.random.uniform(arg_keys[7], (HALF,), jnp.float32, math.log(0.5), math.log(2.0))), 0.5, 2.0),
    }


def phase_tables(shift_offsets, edge_len):
    half_size = edge_len * edge_len // 2
    freq_index = jnp.arange(half_size, dtype=jnp.int32)
    row_freq = freq_index // (edge_len // 2)
    col_freq = freq_index % (edge_len // 2)
    phase_turns = jnp.mod(row_freq[None, :] * shift_offsets[:, 0:1] + col_freq[None, :] * shift_offsets[:, 1:2], edge_len)
    angles = phase_turns.astype(jnp.float32) * (2.0 * jnp.pi / edge_len)
    return jnp.cos(angles), jnp.sin(angles)


def reference(particles, references, slot_class, log_prior, shift_offsets, group_ids, ctf_table, noise_power):
    half_size = L * L // 2
    full_size = 2 * half_size
    inv_noise = 1.0 / noise_power
    cosines, sine_table = phase_tables(shift_offsets, L)
    stacks = references.astype(jnp.float32)
    stack_real = stacks[:, :, :half_size]
    stack_imag = stacks[:, :, half_size:]
    shifted_real = stack_real[:, :, None, :] * cosines[None, None] + stack_imag[:, :, None, :] * sine_table[None, None]
    shifted_imag = stack_imag[:, :, None, :] * cosines[None, None] - stack_real[:, :, None, :] * sine_table[None, None]
    shifted = jnp.concatenate([shifted_real, shifted_imag], axis=3).astype(jnp.bfloat16)
    shifted = lax.optimization_barrier(shifted).astype(jnp.float32).reshape(CLASSES * R * NS, full_size)
    amplitude = (stack_real * stack_real + stack_imag * stack_imag).reshape(CLASSES * R, half_size)
    power_table = ctf_table * ctf_table * inv_noise
    ref_power = jnp.dot(power_table, amplitude.T, precision=lax.Precision.HIGHEST)
    slot_prior = log_prior[slot_class]
    ctf_square = ctf_table * ctf_table
    blocks = particles.reshape(N_GX * N_GY, PART_DEV, L * L)
    group_blocks = group_ids.reshape(N_GX * N_GY, PART_DEV)

    def accumulate(running, inputs):
        moments, group_weights, evidence_sum = running
        pixels, group_rows = inputs
        images = pixels.astype(jnp.float32).reshape(PART_DEV, L, L)
        spectrum = jnp.fft.fft2(images)[:, :, : L // 2] / L
        real_part = jnp.real(spectrum).reshape(PART_DEV, half_size).astype(jnp.float32)
        imag_part = jnp.imag(spectrum).reshape(PART_DEV, half_size).astype(jnp.float32)
        whiten = ctf_table[group_rows] * inv_noise
        weighted = jnp.concatenate([real_part * whiten, imag_part * whiten], axis=1).astype(jnp.bfloat16)
        weighted_wide = weighted.astype(jnp.float32)
        data_power = jnp.sum((real_part * real_part + imag_part * imag_part) * inv_noise, axis=1)
        intersection = jnp.dot(weighted_wide, shifted.T, precision=lax.Precision.HIGHEST)
        own_power = ref_power[group_rows].reshape(PART_DEV, CLASSES, R)
        logits = intersection.reshape(PART_DEV, CLASSES, R, NS) - 0.5 * own_power[:, :, :, None]
        logits = logits - 0.5 * data_power[:, None, None, None] + slot_prior[None, :, None, None]
        logits = logits.reshape(PART_DEV, CLASSES, R * NS)
        row_max = jnp.max(logits, axis=(1, 2), keepdims=True)
        raised = jnp.exp(logits - row_max)
        normaliser = jnp.sum(raised, axis=(1, 2), keepdims=True)
        weights = raised / normaliser
        evidence = row_max[:, 0, 0] + jnp.log(normaliser[:, 0, 0])
        weights_low = weights.astype(jnp.bfloat16).astype(jnp.float32).reshape(PART_DEV, CLASSES * R * NS)
        moments = moments + jnp.dot(weights_low.T, weighted_wide, precision=lax.Precision.HIGHEST)
        group_hot = (group_rows[:, None] == jnp.arange(G, dtype=jnp.int32)[None, :]).astype(jnp.float32)
        group_weights = group_weights + jnp.dot(jnp.sum(weights, axis=2).T, group_hot, precision=lax.Precision.HIGHEST)
        evidence_sum = evidence_sum + jnp.sum(evidence)
        return (moments, group_weights, evidence_sum), None

    start = (jnp.zeros((CLASSES * R * NS, full_size), jnp.float32), jnp.zeros((CLASSES, G), jnp.float32), jnp.zeros((), jnp.float32))
    (moments, group_weights, evidence_sum), unused = lax.scan(accumulate, start, (blocks, group_blocks))
    moments = moments.reshape(CLASSES, R, NS, full_size)
    moment_real = moments[..., :half_size]
    moment_imag = moments[..., half_size:]
    back_real = jnp.sum(moment_real * cosines[None, None] - moment_imag * sine_table[None, None], axis=2)
    back_imag = jnp.sum(moment_imag * cosines[None, None] + moment_real * sine_table[None, None], axis=2)
    class_sums = jnp.concatenate([back_real, back_imag], axis=2)
    ctf_power = jnp.dot(group_weights, ctf_square, precision=lax.Precision.HIGHEST)
    log_evidence = evidence_sum / (PARTICLES * half_size)
    return (class_sums, ctf_power, log_evidence)
```

```python
import functools

import jax
import jax.numpy as jnp
import ml_dtypes
import numpy as np
from jax import lax
from jax.experimental import pallas as pl
from jax.experimental.pallas import tpu as pltpu
from jax.sharding import PartitionSpec as P

L = 64
R = 12
NS = 8
G = 128
HALF = 2048
FR = 4096
PD = 64
NZ = 16
NC = 16
KR = R * NZ
BF = jnp.bfloat16
F32 = jnp.float32
MESH = pl.DeviceIdType.MESH


def dft_tables():
    y2, x = np.divmod(np.arange(512), 64)
    low, v = np.divmod(np.arange(256), 32)
    turns = (8 * y2[:, None] * low[None] + x[:, None] * v[None]) % 64
    angle = turns * (2.0 * np.pi / 64)
    table = np.concatenate([np.cos(angle), -np.sin(angle)], axis=1) / 64
    high = table.astype(ml_dtypes.bfloat16)
    rest = (table - high.astype(np.float64)).astype(ml_dtypes.bfloat16)
    twist = (np.arange(8)[:, None] * low[None]) * (2.0 * np.pi / 64)
    twiddle = np.stack([np.cos(twist), -np.sin(twist)]).astype(np.float32)
    return np.stack([high, rest]), twiddle


def c_add(a, b):
    return a[0] + b[0], a[1] + b[1]


def c_sub(a, b):
    return a[0] - b[0], a[1] - b[1]


def c_mul(a, b):
    return a[0] * b[0] - a[1] * b[1], a[0] * b[1] + a[1] * b[0]


def minus_i(a):
    return a[1], -a[0]


def dft8(a):
    root = np.float32(np.sqrt(0.5))
    s = [c_add(a[n], a[n + 4]) for n in range(4)]
    d = [c_sub(a[n], a[n + 4]) for n in range(4)]
    even, odd = c_add(s[0], s[2]), c_add(s[1], s[3])
    x0, x4 = c_add(even, odd), c_sub(even, odd)
    even, odd = c_sub(s[0], s[2]), minus_i(c_sub(s[1], s[3]))
    x2, x6 = c_add(even, odd), c_sub(even, odd)
    w1 = [(root * (q[0] + q[1]), root * (q[1] - q[0])) for q in (d[1], d[3])]
    w3 = [(root * (q[1] - q[0]), -root * (q[0] + q[1])) for q in (d[1], d[3])]
    even, odd = c_add(d[0], minus_i(d[2])), c_add(w1[0], w3[1])
    x1, x5 = c_add(even, odd), c_sub(even, odd)
    even, odd = c_sub(d[0], minus_i(d[2])), c_add(w3[0], w1[1])
    x3, x7 = c_add(even, odd), c_sub(even, odd)
    return [x0, x1, x2, x3, x4, x5, x6, x7]


def two_parts(value):
    high = value.astype(BF)
    return high, (value - high.astype(F32)).astype(BF)


def dot_nt(a, b):
    return lax.dot_general(a, b, (((1,), (1,)), ((), ())), preferred_element_type=F32)


def dot_nn(a, b):
    return jnp.dot(a, b, preferred_element_type=F32)


def sine_of(turns):
    t = jnp.bitwise_and(turns, 63)
    half = jnp.bitwise_and(t, 31)
    quarter = jnp.minimum(half, 32 - half)
    a = quarter.astype(F32) * np.float32(np.pi / 32)
    q = a * a
    poly = np.float32(-2.5052108385441720e-08)
    for c in (2.7557319223985893e-06, -1.9841269841269841e-04, 8.3333333333333332e-03, -1.6666666666666666e-01):
        poly = poly * q + np.float32(c)
    value = a + a * (q * poly)
    return jnp.where(t >= 32, -value, value)


def kernel(
    part_hbm, refs, slot_class, log_prior, shifts, ids, ctf_hbm, noise, dft_hbm, twiddle,
    out, ctf_out, ev_out,
    pv, ctf, dft, pd, tt, cosb, sinb, wh, pw, vv, dps, a_all, amph, ampl, acc, wt,
    send_a, a16, recv_a, a32, sbuf, own_s, send_x, recv_x, send_s, recv_s,
    ssum, stage, send_3, recv_3, fin, ctf2,
    load_sem, s_a1, r_a1, s_a2, r_a2, s_a3, r_a3, s_x, r_x, s_s, r_s, s_3, r_3, s_4, r_4, s_5, r_5,
):
    z = lax.axis_index("gx")
    g = lax.axis_index("gy")
    chip, core = g // 2, g % 2
    cx, cy = chip // 4, chip % 4
    mate = 2 * chip + 1 - core

    def ahead(d):
        return ((cx + d // 4) % 4) * 4 + (cy + d % 4) % 4

    def behind(d):
        return ((cx + 4 - d // 4) % 4) * 4 + (cy + 4 - d % 4) % 4

    def send(src, dst, s, r, to):
        pltpu.make_async_remote_copy(
            src_ref=src, dst_ref=dst, send_sem=s, recv_sem=r, device_id=to, device_id_type=MESH
        ).start()

    def wait(ref, sem):
        pltpu.make_async_copy(ref, ref, sem).wait()

    def loop(lo, hi, body):
        def step(i, carry):
            body(i)
            return carry

        lax.fori_loop(lo, hi, step, 0)

    def lanes(index, width=128):
        return pl.ds(pl.multiple_of(index * width, width), width)

    loads = [
        pltpu.make_async_copy(ctf_hbm, ctf, load_sem.at[0]),
        pltpu.make_async_copy(part_hbm, pv, load_sem.at[1]),
        pltpu.make_async_copy(dft_hbm, dft, load_sem.at[2]),
    ]
    for load in loads:
        load.start()

    barrier = pltpu.get_barrier_semaphore()

    def greet(d):
        pl.semaphore_signal(barrier, inc=1, device_id=((z + d) % NZ, g), device_id_type=MESH)
        pl.semaphore_signal(barrier, inc=1, device_id=(z, 2 * ahead(d) + core), device_id_type=MESH)

    loop(1, 16, greet)
    pl.semaphore_signal(barrier, inc=1, device_id=(z, mate), device_id_type=MESH)

    a16[...] = jnp.zeros((16, 128), F32)
    a16[0:R, :] = refs[0, :, lanes(core * 16 + chip)].astype(F32)
    send_a[...] = a16[...].astype(BF)
    pl.semaphore_wait(barrier, 31)

    def start_a1(d):
        to = (z + d) % NZ
        send(send_a, recv_a.at[z], s_a1, r_a1, (to, g))

    loop(1, 16, start_a1)
    recv_a[pl.ds(z, 1)] = send_a[...][None]

    freq = lax.broadcasted_iota(jnp.int32, (NS, HALF), 1)
    turns = (freq // 32) * shifts[:, 0:1] + (freq % 32) * shifts[:, 1:2]
    cosb[...] = sine_of(turns + 16)
    sinb[...] = sine_of(turns)
    inv_noise = 1.0 / noise[...]
    hot_t = (lax.broadcasted_iota(jnp.int32, (G, PD), 0) == ids[...]).astype(F32)
    hot = hot_t.T.astype(BF)
    loads[0].wait()
    table_high, table_low = two_parts(ctf[...])
    rows = dot_nn(hot, table_high) + dot_nn(hot, table_low)
    wh[...] = rows * inv_noise
    power_high, power_low = two_parts(rows * rows * inv_noise)
    pw[0:PD, :] = power_high
    pw[PD : 2 * PD, :] = power_low
    square_high, square_low = two_parts(ctf[...] * ctf[...])
    ctf2[0:G, :] = square_high
    ctf2[G : 2 * G, :] = square_low

    wait(recv_a.at[pl.ds(0, 15)], r_a1)
    for k in range(NZ):
        a32[pl.ds(k, R, stride=NZ), :] = recv_a[k].astype(F32)[0:R]
    a_all[:, lanes(g)] = a32[...].astype(BF)
    mine = a_all.at[:, lanes(g)]

    def start_a2(d):
        send(mine, mine, s_a2, r_a2.at[d], (z, 2 * ahead(d) + core))

    loop(1, 16, start_a2)
    send(mine, mine, s_a3, r_a3, (z, mate))

    lane = lax.broadcasted_iota(jnp.int32, (PD, 128), 1)
    loads[1].wait()
    for q in range(4):
        for r in range(4):
            a = pv[:, (q + 8 * r) * 128 : (q + 8 * r + 1) * 128].astype(F32)
            b = pv[:, (q + 8 * r + 4) * 128 : (q + 8 * r + 5) * 128].astype(F32)
            first = jnp.where(lane < 64, a, pltpu.roll(b, 64, 1))
            second = jnp.where(lane < 64, pltpu.roll(a, 64, 1), b)
            cols = slice(r * 128, (r + 1) * 128)
            pd[2 * q * PD : (2 * q + 1) * PD, cols] = first.astype(BF)
            pd[(2 * q + 1) * PD : (2 * q + 2) * PD, cols] = second.astype(BF)
    loads[2].wait()
    tt[...] = dot_nn(pd[...], dft[0]) + dot_nn(pd[...], dft[1])

    def spectrum(pb):
        at = pl.multiple_of(pb * 16, 16)
        power = jnp.zeros((16, 128), F32)
        for h in range(2):
            cols = slice(h * 128, (h + 1) * 128)
            terms = []
            for y1 in range(8):
                where = pl.ds(pl.multiple_of(y1 * PD + at, 16), 16)
                t = tt[where, h * 128 : h * 128 + 128], tt[where, 256 + h * 128 : 256 + h * 128 + 128]
                if y1:
                    t = c_mul(t, (twiddle[0, y1 : y1 + 1, cols], twiddle[1, y1 : y1 + 1, cols]))
                terms.append(t)
            for m, (re, im) in enumerate(dft8(terms)):
                block = 2 * m + h
                f = slice(block * 128, block * 128 + 128)
                power = power + (re * re + im * im) * (1.0 / noise[:, f])
                factor = wh[pl.ds(at, 16), f]
                re, im = re * factor, im * factor
                for s in range(NS):
                    c, n = cosb[s : s + 1, f], sinb[s : s + 1, f]
                    where = pl.ds(pl.multiple_of(s * PD + at, 16), 16)
                    vv[where, block * 256 : block * 256 + 128] = (re * c - im * n).astype(BF)
                    vv[where, block * 256 + 128 : block * 256 + 256] = (re * n + im * c).astype(BF)
        dps[pl.ds(at, 16), :] = power

    loop(0, 4, spectrum)

    slot = lax.broadcasted_iota(jnp.int32, (1, KR), 1) % NZ
    prior = jnp.zeros((1, KR), F32)
    for k in range(NZ):
        prior = jnp.where(slot == k, log_prior[slot_class[k]], prior)

    def forward(d):
        block = a_all.at[:, lanes(2 * behind(d) + core)]
        wait(block, r_a2.at[d])
        send(block, block, s_a3, r_a3, (z, mate))

    loop(1, 16, forward)
    wait(a_all.at[:, pl.ds(0, HALF)], r_a3)

    def amplitude(b):
        both = a_all[:, lanes(b, 256)].astype(F32)
        re, im = both[:, :128], both[:, 128:]
        high, low = two_parts(re * re + im * im)
        amph[:, lanes(b)] = high
        ampl[:, lanes(b)] = low

    loop(0, 16, amplitude)
    both = dot_nt(pw[...], amph[...])
    own_power = both[0:PD] + both[PD : 2 * PD] + dot_nt(pw[0:PD, :], ampl[...])
    base = prior - 0.5 * own_power
    acc[...] = dot_nt(vv[...], a_all[...])

    top = jnp.full((PD, KR), -jnp.inf, F32)
    for s in range(NS):
        value = acc[s * PD : (s + 1) * PD, :] + base
        acc[s * PD : (s + 1) * PD, :] = value
        top = jnp.maximum(top, value)
    top = jnp.max(top, axis=1, keepdims=True)
    total = jnp.zeros((PD, KR), F32)
    for s in range(NS):
        value = jnp.exp(acc[s * PD : (s + 1) * PD, :] - top)
        acc[s * PD : (s + 1) * PD, :] = value
        total = total + value
    total = jnp.sum(total, axis=1, keepdims=True)
    scale = 1.0 / total
    data_power = jnp.sum(dps[...], axis=1, keepdims=True)
    evidence = top + jnp.log(total) - 0.5 * data_power
    evidence = jnp.sum(evidence, axis=0, keepdims=True)
    scale2 = jnp.concatenate([scale, scale], axis=0)
    for s in range(NS // 2):
        w = acc[s * 128 : (s + 1) * 128, :] * scale2
        wt[:, s * 128 : (s + 1) * 128] = w.T.astype(BF)

    hot8 = jnp.concatenate([hot] * NS, axis=0)
    by_group = dot_nn(wt[...], hot8)
    groups = by_group[0:NZ]
    for r in range(1, R):
        groups = groups + by_group[r * NZ : (r + 1) * NZ]

    def block_at(i):
        return ahead((i + 1) % 16)

    def moment(i):
        b = block_at(i)
        part = dot_nn(wt[...], vv[:, lanes(b, 256)])
        sbuf[0] = part[:, :128]
        sbuf[1] = part[:, 128:]
        own_s[b] = sbuf[core]
        send_x[b] = sbuf[1 - core].astype(BF)
        send(send_x.at[b], recv_x.at[b], s_x, r_x.at[b], (z, mate))

    def pair_sum(i):
        b = block_at(i)
        wait(recv_x.at[b], r_x.at[b])
        return (own_s[b] + recv_x[b].astype(F32)).astype(BF), b

    def plane(i):
        value, b = pair_sum(i)
        send_s[b] = value
        send(send_s.at[b], recv_s.at[chip], s_s, r_s, (z, 2 * b + core))

    LAG = 3
    loop(0, LAG, moment)

    def both_steps(i):
        moment(i)
        plane(i - LAG)

    loop(LAG, 16, both_steps)
    loop(16 - LAG, 15, plane)
    value, _ = pair_sum(15)
    recv_s[pl.ds(chip, 1)] = value[None]

    gw_high, gw_low = two_parts(groups)
    ev_high, ev_low = two_parts(evidence)
    for k in range(NZ):
        stage[k, R : R + 1, :] = gw_high[k : k + 1].astype(F32)
        stage[k, R + 1 : R + 2, :] = gw_low[k : k + 1].astype(F32)
        stage[k, R + 2 : R + 3, :] = jnp.broadcast_to(ev_high.astype(F32), (1, 128))
        stage[k, R + 3 : R + 4, :] = jnp.broadcast_to(ev_low.astype(F32), (1, 128))

    wait(recv_s.at[pl.ds(0, 15)], r_s)
    total_s = recv_s[0].astype(F32)
    for t in range(1, NC):
        total_s = total_s + recv_s[t].astype(F32)
    ssum[...] = total_s
    for k in range(NZ):
        stage[k, 0:R, :] = ssum[pl.ds(k, R, stride=NZ), :]
    send_3[...] = stage[...].astype(BF)

    def start_3(d):
        to = (z + d) % NZ
        send(send_3.at[to], recv_3.at[z], s_3, r_3, (to, g))

    loop(1, 16, start_3)
    recv_3[pl.ds(z, 1)] = send_3[pl.ds(z, 1)]
    wait(recv_3.at[pl.ds(0, 15)], r_3)
    last = recv_3[0].astype(F32)
    for t in range(1, NZ):
        last = last + recv_3[t].astype(F32)
    fin[chip, core] = last
    tile = fin.at[chip, core]
    send(tile, tile, s_4, r_4, (z, mate))
    wait(tile, r_4)
    pair = fin.at[chip]

    def start_5(d):
        send(pair, pair, s_5, r_5, (z, 2 * ahead(d) + core))

    loop(1, 16, start_5)
    wait(fin.at[pl.ds(0, 15)], r_5)

    rest = jnp.zeros((R - 8, 128), F32)
    for t in range(NC):
        for c in range(2):
            at = c * HALF + t * 128
            out[0, :, at : at + 128] = fin[t, c, 0:R, :]
            rest = rest + fin[t, c, R:16, :]
    gw_high, gw_low = two_parts(rest[0:1] + rest[1:2])
    left = jnp.concatenate([gw_high, gw_high], axis=1), jnp.concatenate([gw_low, gw_low], axis=1)
    ctf_out[...] = dot_nn(left[0], ctf2[...]) + dot_nn(left[1], ctf2[...])
    ev_out[...] = (rest[2:3] + rest[3:4]) * (1.0 / (PD * NZ * NC * 2 * HALF))

    wait(recv_a.at[pl.ds(0, 15)], s_a1)
    wait(a_all.at[:, pl.ds(0, 15 * 128)], s_a2)
    wait(a_all.at[:, pl.ds(0, HALF)], s_a3)
    wait(send_x, s_x)
    wait(send_s.at[pl.ds(0, 15)], s_s)
    wait(send_3.at[pl.ds(0, 15)], s_3)
    wait(tile, s_4)
    wait(fin.at[pl.ds(0, 15)], s_5)


def shards(dft, twiddle, particles, references, slot_class, log_prior, shift_offsets, group_ids, ctf_table, noise_power):
    vmem = pl.BlockSpec(memory_space=pltpu.VMEM)
    smem = pl.BlockSpec(memory_space=pltpu.SMEM)
    hbm = pl.BlockSpec(memory_space=pl.ANY)
    dma = pltpu.SemaphoreType.DMA
    class_sums, ctf_power, evidence = pl.pallas_call(
        kernel,
        out_shape=(
            jax.ShapeDtypeStruct((1, R, FR), F32),
            jax.ShapeDtypeStruct((1, HALF), F32),
            jax.ShapeDtypeStruct((1, 128), F32),
        ),
        in_specs=[hbm, vmem, smem, smem, vmem, vmem, hbm, vmem, hbm, vmem],
        out_specs=(vmem, vmem, vmem),
        scratch_shapes=[
            pltpu.VMEM((PD, FR), BF),
            pltpu.VMEM((G, HALF), F32),
            pltpu.VMEM((2, 512, 512), BF),
            pltpu.VMEM((512, 512), BF),
            pltpu.VMEM((512, 512), F32),
            pltpu.VMEM((NS, HALF), F32),
            pltpu.VMEM((NS, HALF), F32),
            pltpu.VMEM((PD, HALF), F32),
            pltpu.VMEM((2 * PD, HALF), BF),
            pltpu.VMEM((NS * PD, FR), BF),
            pltpu.VMEM((PD, 128), F32),
            pltpu.VMEM((KR, FR), BF),
            pltpu.VMEM((KR, HALF), BF),
            pltpu.VMEM((KR, HALF), BF),
            pltpu.VMEM((NS * PD, KR), F32),
            pltpu.VMEM((KR, NS * PD), BF),
            pltpu.VMEM((16, 128), BF),
            pltpu.VMEM((16, 128), F32),
            pltpu.VMEM((NZ, 16, 128), BF),
            pltpu.VMEM((KR, 128), F32),
            pltpu.VMEM((2, KR, 128), F32),
            pltpu.VMEM((NC, KR, 128), F32),
            pltpu.VMEM((NC, KR, 128), BF),
            pltpu.VMEM((NC, KR, 128), BF),
            pltpu.VMEM((NC, KR, 128), BF),
            pltpu.VMEM((NC, KR, 128), BF),
            pltpu.VMEM((KR, 128), F32),
            pltpu.VMEM((NZ, 16, 128), F32),
            pltpu.VMEM((NZ, 16, 128), BF),
            pltpu.VMEM((NZ, 16, 128), BF),
            pltpu.VMEM((NC, 2, 16, 128), F32),
            pltpu.VMEM((2 * G, HALF), BF),
            dma((3,)),
            dma, dma,
            dma, dma((16,)),
            dma, dma,
            dma, dma((16,)),
            dma, dma,
            dma, dma,
            dma, dma,
            dma, dma,
        ],
        compiler_params=pltpu.CompilerParams(
            collective_id=0, has_side_effects=True, vmem_limit_bytes=56 * 1024 * 1024
        ),
    )(
        particles, references, slot_class, log_prior, shift_offsets,
        group_ids.reshape(1, PD), ctf_table, noise_power.reshape(1, HALF), dft, twiddle,
    )
    return class_sums, ctf_power, evidence[0, 0]


def solution(mesh):
    dft, twiddle = dft_tables()
    split = ("gx", "gy")
    in_specs = (P(split, None), P("gx", None, None), P(), P(), P(), P(split), P(), P())
    out_specs = (P("gx", None, None), P("gx", None), P())

    def run(*args):
        body = functools.partial(shards, jnp.asarray(dft), jnp.asarray(twiddle))
        return jax.shard_map(body, mesh=mesh, in_specs=in_specs, out_specs=out_specs, check_vma=False)(*args)

    return run
```

```python
import functools

import jax
import jax.numpy as jnp
import ml_dtypes
import numpy as np
from jax import lax
from jax.experimental import pallas as pl
from jax.experimental.pallas import tpu as pltpu
from jax.sharding import PartitionSpec as P

L = 64
R = 12
NS = 8
G = 128
HALF = 2048
FR = 4096
PD = 64
NZ = 16
NC = 16
HAND_LAG = 3
LAG = 4
KR = R * NZ
BF = jnp.bfloat16
F32 = jnp.float32
MESH = pl.DeviceIdType.MESH


def dft_tables():
    y2, x = np.divmod(np.arange(512), 64)
    low, v = np.divmod(np.arange(256), 32)
    turns = (8 * y2[:, None] * low[None] + x[:, None] * v[None]) % 64
    angle = turns * (2.0 * np.pi / 64)
    table = np.concatenate([np.cos(angle), -np.sin(angle)], axis=1) / 64
    high = table.astype(ml_dtypes.bfloat16)
    rest = (table - high.astype(np.float64)).astype(ml_dtypes.bfloat16)
    twist = (np.arange(8)[:, None] * low[None]) * (2.0 * np.pi / 64)
    twiddle = np.stack([np.cos(twist), -np.sin(twist)]).astype(np.float32)
    return np.stack([high, rest]), twiddle


def c_add(a, b):
    return a[0] + b[0], a[1] + b[1]


def c_sub(a, b):
    return a[0] - b[0], a[1] - b[1]


def c_mul(a, b):
    return a[0] * b[0] - a[1] * b[1], a[0] * b[1] + a[1] * b[0]


def minus_i(a):
    return a[1], -a[0]


def dft8(a):
    root = np.float32(np.sqrt(0.5))
    s = [c_add(a[n], a[n + 4]) for n in range(4)]
    d = [c_sub(a[n], a[n + 4]) for n in range(4)]
    even, odd = c_add(s[0], s[2]), c_add(s[1], s[3])
    x0, x4 = c_add(even, odd), c_sub(even, odd)
    even, odd = c_sub(s[0], s[2]), minus_i(c_sub(s[1], s[3]))
    x2, x6 = c_add(even, odd), c_sub(even, odd)
    w1 = [(root * (q[0] + q[1]), root * (q[1] - q[0])) for q in (d[1], d[3])]
    w3 = [(root * (q[1] - q[0]), -root * (q[0] + q[1])) for q in (d[1], d[3])]
    even, odd = c_add(d[0], minus_i(d[2])), c_add(w1[0], w3[1])
    x1, x5 = c_add(even, odd), c_sub(even, odd)
    even, odd = c_sub(d[0], minus_i(d[2])), c_add(w3[0], w1[1])
    x3, x7 = c_add(even, odd), c_sub(even, odd)
    return [x0, x1, x2, x3, x4, x5, x6, x7]


def two_parts(value):
    high = value.astype(BF)
    return high, (value - high.astype(F32)).astype(BF)


def dot_nt(a, b):
    return lax.dot_general(a, b, (((1,), (1,)), ((), ())), preferred_element_type=F32)


def dot_nn(a, b):
    return jnp.dot(a, b, preferred_element_type=F32)


def sine_of(turns):
    t = jnp.bitwise_and(turns, 63)
    half = jnp.bitwise_and(t, 31)
    quarter = jnp.minimum(half, 32 - half)
    a = quarter.astype(F32) * np.float32(np.pi / 32)
    q = a * a
    poly = np.float32(-2.5052108385441720e-08)
    for c in (2.7557319223985893e-06, -1.9841269841269841e-04, 8.3333333333333332e-03, -1.6666666666666666e-01):
        poly = poly * q + np.float32(c)
    value = a + a * (q * poly)
    return jnp.where(t >= 32, -value, value)


def kernel(
    part_hbm, refs, slot_class, log_prior, shifts, ids, ctf_hbm, noise, dft_hbm, twiddle,
    out, ctf_out, ev_out,
    pv, ctf, dft, pd, tt, cosb, sinb, wh, pw, vv, dps, a_all, power, acc, wt,
    send_a, a16, recv_a, a32, sbuf, own_s, send_x, recv_x, send_s, recv_s,
    ssum, stage, send_3, recv_3, fin, ctf2,
    load_sem, s_a1, r_a1, s_a2, r_a2, s_a3, r_a3, s_x, r_x, s_s, r_s, s_3, r_3, s_5, r_5,
):
    z = lax.axis_index("gx")
    g = lax.axis_index("gy")
    chip, core = g // 2, g % 2
    cx, cy = chip // 4, chip % 4
    mate = 2 * chip + 1 - core

    def ahead(d):
        return ((cx + d // 4) % 4) * 4 + (cy + d % 4) % 4

    def behind(d):
        return ((cx + 4 - d // 4) % 4) * 4 + (cy + 4 - d % 4) % 4

    def send(src, dst, s, r, to):
        pltpu.make_async_remote_copy(
            src_ref=src, dst_ref=dst, send_sem=s, recv_sem=r, device_id=to, device_id_type=MESH
        ).start()

    def wait(ref, sem):
        pltpu.make_async_copy(ref, ref, sem).wait()

    def loop(lo, hi, body):
        def step(i, carry):
            body(i)
            return carry

        lax.fori_loop(lo, hi, step, 0)

    def lanes(index, width=128):
        return pl.ds(pl.multiple_of(index * width, width), width)

    loads = [
        pltpu.make_async_copy(ctf_hbm, ctf, load_sem.at[0]),
        pltpu.make_async_copy(part_hbm, pv, load_sem.at[1]),
        pltpu.make_async_copy(dft_hbm, dft, load_sem.at[2]),
    ]
    for load in loads:
        load.start()

    barrier = pltpu.get_barrier_semaphore()

    def greet(d):
        pl.semaphore_signal(barrier, inc=1, device_id=((z + d) % NZ, g), device_id_type=MESH)
        pl.semaphore_signal(barrier, inc=1, device_id=(z, 2 * ahead(d)), device_id_type=MESH)
        pl.semaphore_signal(barrier, inc=1, device_id=(z, 2 * ahead(d) + 1), device_id_type=MESH)

    loop(1, 16, greet)
    pl.semaphore_signal(barrier, inc=1, device_id=(z, mate), device_id_type=MESH)

    a16[...] = jnp.zeros((16, 128), F32)
    a16[0:R, :] = refs[0, :, lanes(core * 16 + chip)].astype(F32)
    send_a[...] = a16[...].astype(BF)
    pl.semaphore_wait(barrier, 46)

    def start_a1(d):
        to = (z + d) % NZ
        send(send_a, recv_a.at[z], s_a1, r_a1, (to, g))

    loop(1, 16, start_a1)
    recv_a[pl.ds(z, 1)] = send_a[...][None]

    freq = lax.broadcasted_iota(jnp.int32, (NS, HALF), 1)
    which = lax.broadcasted_iota(jnp.int32, (NS, 128), 0)
    down, along = jnp.zeros((NS, 128), jnp.int32), jnp.zeros((NS, 128), jnp.int32)
    for s in range(NS):
        down = jnp.where(which == s, shifts[0, s], down)
        along = jnp.where(which == s, shifts[1, s], along)
    turns = (freq // 32) * down[:, 0:1] + (freq % 32) * along[:, 0:1]
    cosb[...] = sine_of(turns + 16)
    sinb[...] = sine_of(turns)
    inv_noise = 1.0 / noise[...]
    hot_t = (lax.broadcasted_iota(jnp.int32, (G, PD), 0) == ids[...]).astype(F32)
    hot = hot_t.T.astype(BF)
    loads[0].wait()
    table_high, table_low = two_parts(ctf[...])
    rows = dot_nn(hot, table_high) + dot_nn(hot, table_low)
    wh[...] = rows * inv_noise
    power_high, power_low = two_parts(rows * rows * inv_noise)
    pw[0:PD, :] = power_high
    pw[PD : 2 * PD, :] = power_low
    square_high, square_low = two_parts(ctf[...] * ctf[...])
    ctf2[0:G, :] = square_high
    ctf2[G : 2 * G, :] = square_low

    wait(recv_a.at[pl.ds(0, 15)], r_a1)
    for k in range(NZ):
        a32[pl.ds(k, R, stride=NZ), :] = recv_a[k].astype(F32)[0:R]
    a_all[:, lanes(g)] = a32[...].astype(BF)
    mine = a_all.at[:, lanes(g)]

    def start_a2(d):
        send(mine, mine, s_a2, r_a2.at[d], (z, 2 * ahead(d) + core))

    loop(1, 16, start_a2)
    send(mine, mine, s_a3, r_a3.at[0], (z, mate))

    lane = lax.broadcasted_iota(jnp.int32, (PD, 128), 1)
    loads[1].wait()
    for q in range(4):
        for r in range(4):
            a = pv[:, (q + 8 * r) * 128 : (q + 8 * r + 1) * 128].astype(F32)
            b = pv[:, (q + 8 * r + 4) * 128 : (q + 8 * r + 5) * 128].astype(F32)
            first = jnp.where(lane < 64, a, pltpu.roll(b, 64, 1))
            second = jnp.where(lane < 64, pltpu.roll(a, 64, 1), b)
            cols = slice(r * 128, (r + 1) * 128)
            pd[2 * q * PD : (2 * q + 1) * PD, cols] = first.astype(BF)
            pd[(2 * q + 1) * PD : (2 * q + 2) * PD, cols] = second.astype(BF)
    loads[2].wait()
    tt[...] = dot_nn(pd[...], dft[0]) + dot_nn(pd[...], dft[1])

    def spectrum(pb):
        at = pl.multiple_of(pb * 16, 16)
        total = jnp.zeros((16, 128), F32)
        for h in range(2):
            cols = slice(h * 128, (h + 1) * 128)
            terms = []
            for y1 in range(8):
                where = pl.ds(pl.multiple_of(y1 * PD + at, 16), 16)
                t = tt[where, h * 128 : h * 128 + 128], tt[where, 256 + h * 128 : 256 + h * 128 + 128]
                if y1:
                    t = c_mul(t, (twiddle[0, y1 : y1 + 1, cols], twiddle[1, y1 : y1 + 1, cols]))
                terms.append(t)
            for m, (re, im) in enumerate(dft8(terms)):
                block = 2 * m + h
                f = slice(block * 128, block * 128 + 128)
                total = total + (re * re + im * im) * (1.0 / noise[:, f])
                factor = wh[pl.ds(at, 16), f]
                re, im = re * factor, im * factor
                for s in range(NS):
                    c, n = cosb[s : s + 1, f], sinb[s : s + 1, f]
                    where = pl.ds(pl.multiple_of(s * PD + at, 16), 16)
                    vv[where, block * 256 : block * 256 + 128] = (re * c - im * n).astype(BF)
                    vv[where, block * 256 + 128 : block * 256 + 256] = (re * n + im * c).astype(BF)
        dps[pl.ds(at, 16), :] = total

    loop(0, 4, spectrum)

    slot = lax.broadcasted_iota(jnp.int32, (1, KR), 1) % NZ
    prior = jnp.zeros((1, KR), F32)
    for k in range(NZ):
        prior = jnp.where(slot == k, log_prior[slot_class[k]], prior)

    acc[...] = jnp.zeros((NS * PD, KR), F32)
    power[...] = jnp.zeros((2 * PD, KR), F32)

    def forward(d):
        block = a_all.at[:, lanes(2 * behind(d) + core)]
        wait(block, r_a2.at[d])
        send(block, block, s_a3, r_a3.at[d], (z, mate))

    def score(d):
        b = behind(d)
        wait(a_all.at[:, lanes(2 * b + 1 - core)], r_a3.at[d])
        both = a_all[:, lanes(b, 256)]
        acc[...] += dot_nt(vv[:, lanes(b, 256)], both)
        re, im = both[:, :128].astype(F32), both[:, 128:].astype(F32)
        high, low = two_parts(re * re + im * im)
        power[...] += dot_nt(pw[:, lanes(b)], high)
        power[0:PD, :] += dot_nt(pw[0:PD, lanes(b)], low)

    def forward_score(d):
        forward(d)
        score(d - HAND_LAG)

    loop(1, HAND_LAG, forward)
    loop(HAND_LAG, 16, forward_score)
    loop(16 - HAND_LAG, 16, score)
    base = prior - 0.5 * (power[0:PD, :] + power[PD : 2 * PD, :])

    top = jnp.full((PD, KR), -jnp.inf, F32)
    for s in range(NS):
        value = acc[s * PD : (s + 1) * PD, :] + base
        acc[s * PD : (s + 1) * PD, :] = value
        top = jnp.maximum(top, value)
    top = jnp.max(top, axis=1, keepdims=True)
    total = jnp.zeros((PD, KR), F32)
    for s in range(NS):
        value = jnp.exp(acc[s * PD : (s + 1) * PD, :] - top)
        acc[s * PD : (s + 1) * PD, :] = value
        total = total + value
    total = jnp.sum(total, axis=1, keepdims=True)
    scale = 1.0 / total
    data_power = jnp.sum(dps[...], axis=1, keepdims=True)
    evidence = top + jnp.log(total) - 0.5 * data_power
    evidence = jnp.sum(evidence, axis=0, keepdims=True)
    scale2 = jnp.concatenate([scale, scale], axis=0)
    for s in range(NS // 2):
        w = acc[s * 128 : (s + 1) * 128, :] * scale2
        wt[:, s * 128 : (s + 1) * 128] = w.T.astype(BF)

    def block_at(i):
        return ahead((i + 1) % 16)

    def moment(i):
        b = block_at(i)
        part = dot_nn(wt[...], vv[:, lanes(b, 256)])
        sbuf[0] = part[:, :128]
        sbuf[1] = part[:, 128:]
        own_s[b] = sbuf[core]
        send_x[b] = sbuf[1 - core].astype(BF)
        send(send_x.at[b], recv_x.at[b], s_x, r_x.at[b], (z, mate))

    def pair_sum(i):
        b = block_at(i)
        wait(recv_x.at[b], r_x.at[b])
        return (own_s[b] + recv_x[b].astype(F32)).astype(BF), b

    def plane(i):
        value, b = pair_sum(i)
        send_s[b] = value
        send(send_s.at[b], recv_s.at[chip], s_s, r_s, (z, 2 * b + core))

    loop(0, LAG, moment)

    def both_steps(i):
        moment(i)
        plane(i - LAG)

    loop(LAG, 16, both_steps)
    loop(16 - LAG, 15, plane)
    value, _ = pair_sum(15)
    recv_s[pl.ds(chip, 1)] = value[None]

    hot8 = jnp.concatenate([hot] * NS, axis=0)
    by_group = dot_nn(wt[...], hot8)
    groups = by_group[0:NZ]
    for r in range(1, R):
        groups = groups + by_group[r * NZ : (r + 1) * NZ]
    gw_high, gw_low = two_parts(groups)
    ev_high, ev_low = two_parts(evidence)
    for k in range(NZ):
        stage[k, R : R + 1, :] = gw_high[k : k + 1].astype(F32)
        stage[k, R + 1 : R + 2, :] = gw_low[k : k + 1].astype(F32)
        stage[k, R + 2 : R + 3, :] = jnp.broadcast_to(ev_high.astype(F32), (1, 128))
        stage[k, R + 3 : R + 4, :] = jnp.broadcast_to(ev_low.astype(F32), (1, 128))

    wait(recv_s.at[pl.ds(0, 15)], r_s)
    total_s = recv_s[0].astype(F32)
    for t in range(1, NC):
        total_s = total_s + recv_s[t].astype(F32)
    ssum[...] = total_s
    for k in range(NZ):
        stage[k, 0:R, :] = ssum[pl.ds(k, R, stride=NZ), :]
    send_3[...] = stage[...].astype(BF)

    def start_3(d):
        to = (z + d) % NZ
        send(send_3.at[to], recv_3.at[z], s_3, r_3, (to, g))

    loop(1, 16, start_3)
    recv_3[pl.ds(z, 1)] = send_3[pl.ds(z, 1)]
    wait(recv_3.at[pl.ds(0, 15)], r_3)
    last = recv_3[0].astype(F32)
    for t in range(1, NZ):
        last = last + recv_3[t].astype(F32)
    a16[...] = last
    for row in (R, R + 2):
        high, low = two_parts(last[row : row + 1] + last[row + 1 : row + 2])
        a16[row : row + 1, :] = high.astype(F32)
        a16[row + 1 : row + 2, :] = low.astype(F32)
    fin[pl.ds(g, 1)] = a16[...].astype(BF)[None]
    tile = fin.at[g]

    def start_5(d):
        for c in range(2):
            send(tile, tile, s_5, r_5, (z, 2 * ahead(d) + c))

    loop(1, 16, start_5)
    send(tile, tile, s_5, r_5, (z, mate))
    wait(fin.at[pl.ds(0, 31)], r_5)

    rest = jnp.zeros((R - 8, 128), F32)
    for t in range(NC):
        for c in range(2):
            at = c * HALF + t * 128
            block = fin[2 * t + c].astype(F32)
            out[:, 0, at : at + 128] = block[0:R]
            rest = rest + block[R:16]
    gw_high, gw_low = two_parts(rest[0:1] + rest[1:2])
    left = jnp.concatenate([gw_high, gw_high], axis=1), jnp.concatenate([gw_low, gw_low], axis=1)
    ctf_out[...] = dot_nn(left[0], ctf2[...]) + dot_nn(left[1], ctf2[...])
    ev_out[...] = (rest[2:3] + rest[3:4]) * (1.0 / (PD * NZ * NC * 2 * HALF))

    wait(recv_a.at[pl.ds(0, 15)], s_a1)
    wait(a_all.at[:, pl.ds(0, 15 * 128)], s_a2)
    wait(a_all.at[:, pl.ds(0, HALF)], s_a3)
    wait(send_x, s_x)
    wait(send_s.at[pl.ds(0, 15)], s_s)
    wait(send_3.at[pl.ds(0, 15)], s_3)
    wait(fin.at[pl.ds(0, 31)], s_5)


def shards(dft, twiddle, particles, references, slot_class, log_prior, shift_offsets, group_ids, ctf_table, noise_power):
    vmem = pl.BlockSpec(memory_space=pltpu.VMEM)
    smem = pl.BlockSpec(memory_space=pltpu.SMEM)
    hbm = pl.BlockSpec(memory_space=pl.ANY)
    dma = pltpu.SemaphoreType.DMA
    class_sums, ctf_power, evidence = pl.pallas_call(
        kernel,
        out_shape=(
            jax.ShapeDtypeStruct((R, 1, FR), F32),
            jax.ShapeDtypeStruct((1, HALF), F32),
            jax.ShapeDtypeStruct((1, 128), F32),
        ),
        in_specs=[hbm, vmem, smem, smem, smem, vmem, hbm, vmem, hbm, vmem],
        out_specs=(vmem, vmem, vmem),
        scratch_shapes=[
            pltpu.VMEM((PD, FR), BF),
            pltpu.VMEM((G, HALF), F32),
            pltpu.VMEM((2, 512, 512), BF),
            pltpu.VMEM((512, 512), BF),
            pltpu.VMEM((512, 512), F32),
            pltpu.VMEM((NS, HALF), F32),
            pltpu.VMEM((NS, HALF), F32),
            pltpu.VMEM((PD, HALF), F32),
            pltpu.VMEM((2 * PD, HALF), BF),
            pltpu.VMEM((NS * PD, FR), BF),
            pltpu.VMEM((PD, 128), F32),
            pltpu.VMEM((KR, FR), BF),
            pltpu.VMEM((2 * PD, KR), F32),
            pltpu.VMEM((NS * PD, KR), F32),
            pltpu.VMEM((KR, NS * PD), BF),
            pltpu.VMEM((16, 128), BF),
            pltpu.VMEM((16, 128), F32),
            pltpu.VMEM((NZ, 16, 128), BF),
            pltpu.VMEM((KR, 128), F32),
            pltpu.VMEM((2, KR, 128), F32),
            pltpu.VMEM((NC, KR, 128), F32),
            pltpu.VMEM((NC, KR, 128), BF),
            pltpu.VMEM((NC, KR, 128), BF),
            pltpu.VMEM((NC, KR, 128), BF),
            pltpu.VMEM((NC, KR, 128), BF),
            pltpu.VMEM((KR, 128), F32),
            pltpu.VMEM((NZ, 16, 128), F32),
            pltpu.VMEM((NZ, 16, 128), BF),
            pltpu.VMEM((NZ, 16, 128), BF),
            pltpu.VMEM((2 * NC, 16, 128), BF),
            pltpu.VMEM((2 * G, HALF), BF),
            dma((3,)),
            dma, dma,
            dma, dma((16,)),
            dma, dma((16,)),
            dma, dma((16,)),
            dma, dma,
            dma, dma,
            dma, dma,
        ],
        compiler_params=pltpu.CompilerParams(
            collective_id=0, has_side_effects=True, vmem_limit_bytes=56 * 1024 * 1024
        ),
    )(
        particles, references, slot_class, log_prior, shift_offsets.T,
        group_ids.reshape(1, PD), ctf_table, noise_power.reshape(1, HALF), dft, twiddle,
    )
    return class_sums.transpose(1, 0, 2), ctf_power, evidence[0, 0]


def solution(mesh):
    dft, twiddle = dft_tables()
    split = ("gx", "gy")
    in_specs = (P(split, None), P("gx", None, None), P(), P(), P(), P(split), P(), P())
    out_specs = (P("gx", None, None), P("gx", None), P())

    def run(*args):
        body = functools.partial(shards, jnp.asarray(dft), jnp.asarray(twiddle))
        return jax.shard_map(body, mesh=mesh, in_specs=in_specs, out_specs=out_specs, check_vma=False)(*args)

    return run
```

```python
import functools

import jax
import jax.numpy as jnp
import ml_dtypes
import numpy as np
from jax import lax
from jax.experimental import pallas as pl
from jax.experimental.pallas import tpu as pltpu
from jax.sharding import PartitionSpec as P

L = 64
R = 12
NS = 8
G = 128
HALF = 2048
FR = 4096
PD = 64
NZ = 16
NC = 16
LAG = 4
HR = R * NZ // 2
KR = R * NZ
BF = jnp.bfloat16
F32 = jnp.float32
MESH = pl.DeviceIdType.MESH


def dft_tables():
    y2, x = np.divmod(np.arange(512), 64)
    low, v = np.divmod(np.arange(256), 32)
    turns = (8 * y2[:, None] * low[None] + x[:, None] * v[None]) % 64
    angle = turns * (2.0 * np.pi / 64)
    table = np.concatenate([np.cos(angle), -np.sin(angle)], axis=1) / 64
    high = table.astype(ml_dtypes.bfloat16)
    rest = (table - high.astype(np.float64)).astype(ml_dtypes.bfloat16)
    twist = (np.arange(8)[:, None] * low[None]) * (2.0 * np.pi / 64)
    twiddle = np.stack([np.cos(twist), -np.sin(twist)]).astype(np.float32)
    return np.stack([high, rest]), twiddle


def c_add(a, b):
    return a[0] + b[0], a[1] + b[1]


def c_sub(a, b):
    return a[0] - b[0], a[1] - b[1]


def c_mul(a, b):
    return a[0] * b[0] - a[1] * b[1], a[0] * b[1] + a[1] * b[0]


def minus_i(a):
    return a[1], -a[0]


def dft8(a):
    root = np.float32(np.sqrt(0.5))
    s = [c_add(a[n], a[n + 4]) for n in range(4)]
    d = [c_sub(a[n], a[n + 4]) for n in range(4)]
    even, odd = c_add(s[0], s[2]), c_add(s[1], s[3])
    x0, x4 = c_add(even, odd), c_sub(even, odd)
    even, odd = c_sub(s[0], s[2]), minus_i(c_sub(s[1], s[3]))
    x2, x6 = c_add(even, odd), c_sub(even, odd)
    w1 = [(root * (q[0] + q[1]), root * (q[1] - q[0])) for q in (d[1], d[3])]
    w3 = [(root * (q[1] - q[0]), -root * (q[0] + q[1])) for q in (d[1], d[3])]
    even, odd = c_add(d[0], minus_i(d[2])), c_add(w1[0], w3[1])
    x1, x5 = c_add(even, odd), c_sub(even, odd)
    even, odd = c_sub(d[0], minus_i(d[2])), c_add(w3[0], w1[1])
    x3, x7 = c_add(even, odd), c_sub(even, odd)
    return [x0, x1, x2, x3, x4, x5, x6, x7]


def two_parts(value):
    high = value.astype(BF)
    return high, (value - high.astype(F32)).astype(BF)


def dot_nt(a, b):
    return lax.dot_general(a, b, (((1,), (1,)), ((), ())), preferred_element_type=F32)


def dot_nn(a, b):
    return jnp.dot(a, b, preferred_element_type=F32)


def sine_of(turns):
    t = jnp.bitwise_and(turns, 63)
    half = jnp.bitwise_and(t, 31)
    quarter = jnp.minimum(half, 32 - half)
    a = quarter.astype(F32) * np.float32(np.pi / 32)
    q = a * a
    poly = np.float32(-2.5052108385441720e-08)
    for c in (2.7557319223985893e-06, -1.9841269841269841e-04, 8.3333333333333332e-03, -1.6666666666666666e-01):
        poly = poly * q + np.float32(c)
    value = a + a * (q * poly)
    return jnp.where(t >= 32, -value, value)


def kernel(
    part_hbm, refs_hbm, slot_hbm, prior_hbm, shifts_hbm, ids_hbm, ctf_hbm, noise_hbm, dft_hbm, twiddle_hbm,
    fin_out,
    refs, slot_class, log_prior, shifts, ids, noise, twiddle, pv, ctf, dft, pd, tt, cosb, sinb, wh, pw, vv, dps, a_all, power, acc, wt,
    send_a, a16, recv_a, a32, sbuf, own_s, send_x, recv_x, send_s, recv_s, send_b, recv_b,
    ssum, stage, send_3, recv_3, fin,
    load_sem, s_a1, r_a1, s_a2, s_a2b, r_a2, r_a2b, s_a3, r_a3, s_x, r_x, s_s, r_s, s_b, r_b, s_3, r_3, s_5, r_5,
):
    z = lax.axis_index("gx")
    g = lax.axis_index("gy")
    chip, core = g // 2, g % 2
    cx, cy = chip // 4, chip % 4
    mate = 2 * chip + 1 - core

    def ahead(d):
        return ((cx + d // 4) % 4) * 4 + (cy + d % 4) % 4

    def behind(d):
        return ((cx + 4 - d // 4) % 4) * 4 + (cy + 4 - d % 4) % 4

    def send(src, dst, s, r, to):
        pltpu.make_async_remote_copy(
            src_ref=src, dst_ref=dst, send_sem=s, recv_sem=r, device_id=to, device_id_type=MESH
        ).start()

    def wait(ref, sem):
        pltpu.make_async_copy(ref, ref, sem).wait()

    def loop(lo, hi, body):
        def step(i, carry):
            body(i)
            return carry

        lax.fori_loop(lo, hi, step, 0)

    def lanes(index, width=128):
        return pl.ds(pl.multiple_of(index * width, width), width)

    barrier = pltpu.get_barrier_semaphore()

    def greet_z(d):
        pl.semaphore_signal(barrier, inc=1, device_id=((z + d) % NZ, g), device_id_type=MESH)

    def greet_plane(d):
        pl.semaphore_signal(barrier, inc=1, device_id=(z, 2 * ahead(d)), device_id_type=MESH)
        pl.semaphore_signal(barrier, inc=1, device_id=(z, 2 * ahead(d) + 1), device_id_type=MESH)

    loop(1, 16, greet_z)
    loads = [
        pltpu.make_async_copy(src, dst, load_sem.at[n])
        for n, (src, dst) in enumerate(
            (
                (refs_hbm, refs), (shifts_hbm, shifts), (ids_hbm, ids), (noise_hbm, noise), (ctf_hbm, ctf),
                (part_hbm, pv), (dft_hbm, dft), (twiddle_hbm, twiddle), (slot_hbm, slot_class), (prior_hbm, log_prior),
            )
        )
    ]
    for load in loads:
        load.start()
    loop(1, 16, greet_plane)
    pl.semaphore_signal(barrier, inc=1, device_id=(z, mate), device_id_type=MESH)
    for load in loads[:4]:
        load.wait()

    a16[...] = jnp.zeros((16, 128), F32)
    a16[0:R, :] = refs[0, :, lanes(core * 16 + chip)].astype(F32)
    send_a[...] = a16[...].astype(BF)
    freq = lax.broadcasted_iota(jnp.int32, (NS, HALF), 1)
    which = lax.broadcasted_iota(jnp.int32, (NS, 128), 0)
    down, along = jnp.zeros((NS, 128), jnp.int32), jnp.zeros((NS, 128), jnp.int32)
    for s in range(NS):
        down = jnp.where(which == s, shifts[0, s], down)
        along = jnp.where(which == s, shifts[1, s], along)
    turns = (freq // 32) * down[:, 0:1] + (freq % 32) * along[:, 0:1]
    cosb[...] = sine_of(turns + 16)
    sinb[...] = sine_of(turns)
    inv_noise = 1.0 / noise[...]
    hot_t = (lax.broadcasted_iota(jnp.int32, (G, PD), 0) == ids[...]).astype(F32)
    hot = hot_t.T.astype(BF)
    loads[4].wait()
    table_high, table_low = two_parts(ctf[...])
    rows = dot_nn(hot, table_high) + dot_nn(hot, table_low)
    wh[...] = rows * inv_noise
    power_high, power_low = two_parts(rows * rows * inv_noise)
    pw[0:PD, :] = power_high
    pw[PD : 2 * PD, :] = power_low

    pl.semaphore_wait(barrier, 46)

    def start_a1(d):
        to = (z + d) % NZ
        send(send_a, recv_a.at[z], s_a1, r_a1, (to, g))

    loop(1, 16, start_a1)
    recv_a[pl.ds(z, 1)] = send_a[...][None]

    lane = lax.broadcasted_iota(jnp.int32, (PD, 128), 1)
    loads[5].wait()
    for q in range(4):
        for r in range(4):
            a = pv[:, (q + 8 * r) * 128 : (q + 8 * r + 1) * 128].astype(F32)
            b = pv[:, (q + 8 * r + 4) * 128 : (q + 8 * r + 5) * 128].astype(F32)
            first = jnp.where(lane < 64, a, pltpu.roll(b, 64, 1))
            second = jnp.where(lane < 64, pltpu.roll(a, 64, 1), b)
            cols = slice(r * 128, (r + 1) * 128)
            pd[2 * q * PD : (2 * q + 1) * PD, cols] = first.astype(BF)
            pd[(2 * q + 1) * PD : (2 * q + 2) * PD, cols] = second.astype(BF)
    loads[6].wait()
    loads[7].wait()
    tt[...] = dot_nn(pd[...], dft[0]) + dot_nn(pd[...], dft[1])

    def spectrum(pb):
        at = pl.multiple_of(pb * 16, 16)
        total = jnp.zeros((16, 128), F32)
        for h in range(2):
            cols = slice(h * 128, (h + 1) * 128)
            terms = []
            for y1 in range(8):
                where = pl.ds(pl.multiple_of(y1 * PD + at, 16), 16)
                t = tt[where, h * 128 : h * 128 + 128], tt[where, 256 + h * 128 : 256 + h * 128 + 128]
                if y1:
                    t = c_mul(t, (twiddle[0, y1 : y1 + 1, cols], twiddle[1, y1 : y1 + 1, cols]))
                terms.append(t)
            for m, (re, im) in enumerate(dft8(terms)):
                block = 2 * m + h
                f = slice(block * 128, block * 128 + 128)
                total = total + (re * re + im * im) * (1.0 / noise[:, f])
                factor = wh[pl.ds(at, 16), f]
                re, im = re * factor, im * factor
                for s in range(NS):
                    c, n = cosb[s : s + 1, f], sinb[s : s + 1, f]
                    where = pl.ds(pl.multiple_of(s * PD + at, 16), 16)
                    vv[where, block * 256 : block * 256 + 128] = (re * c - im * n).astype(BF)
                    vv[where, block * 256 + 128 : block * 256 + 256] = (re * n + im * c).astype(BF)
        dps[pl.ds(at, 16), :] = total

    loop(0, 4, spectrum)

    loads[8].wait()
    loads[9].wait()
    slot = lax.broadcasted_iota(jnp.int32, (1, KR), 1) % NZ
    prior = jnp.zeros((1, KR), F32)
    for k in range(NZ):
        prior = jnp.where(slot == k, log_prior[slot_class[k]], prior)

    wait(recv_a.at[pl.ds(0, 15)], r_a1)
    for k in range(NZ):
        a32[pl.ds(k, R, stride=NZ), :] = recv_a[k].astype(F32)[0:R]
    a_all[:, lanes(g)] = a32[...].astype(BF)
    mine = a_all.at[:, lanes(g)]

    def start_a2(d):
        send(mine, mine, s_a2, r_a2.at[4 * d], (z, 2 * ahead(4 * d) + core))
        send(mine, mine, s_a2, r_a2.at[d], (z, 2 * ahead(d) + core))

    loop(1, 4, start_a2)
    send(mine, mine, s_a3, r_a3.at[0], (z, mate))

    acc[...] = jnp.zeros((NS * PD, KR), F32)
    power[...] = jnp.zeros((2 * PD, KR), F32)

    def hand_on(block, d):
        send(block, block, s_a3, r_a3.at[d], (z, mate))

    def direct(i):
        for d, rows, first, step in ((4 * i, slice(0, HR), 4 * i, 1), (i, slice(HR, KR), i, 4)):
            at = lanes(2 * behind(d) + core)
            block = a_all.at[:, at]
            wait(block, r_a2.at[d])
            part = a_all.at[rows, at]
            for n in range(1, 4):
                sem = (r_a2 if step == 1 else r_a2b).at[first + n * step]
                send(part, part, s_a2b, sem, (z, 2 * ahead(n * step) + core))
            hand_on(block, d)

    def diagonal(n):
        return (n // 3 + 1) * 4 + n % 3 + 1

    def relayed(n):
        d = diagonal(n)
        at = lanes(2 * behind(d) + core)
        wait(a_all.at[0:HR, at], r_a2.at[d])
        wait(a_all.at[HR:KR, at], r_a2b.at[d])
        hand_on(a_all.at[:, at], d)

    def score(d):
        b = behind(d)
        wait(a_all.at[:, lanes(2 * b + 1 - core)], r_a3.at[d])
        both = a_all[:, lanes(b, 256)]
        acc[...] += dot_nt(vv[:, lanes(b, 256)], both)
        re, im = both[:, :128].astype(F32), both[:, 128:].astype(F32)
        high, low = two_parts(re * re + im * im)
        power[...] += dot_nt(pw[:, lanes(b)], high)
        power[0:PD, :] += dot_nt(pw[0:PD, lanes(b)], low)

    def first_steps(n):
        relayed(n)
        score(4 * (n + 1))
        score(n + 1)

    def next_steps(n):
        relayed(n)
        score(diagonal(n - 3))

    loop(1, 4, direct)
    score(0)
    loop(0, 3, first_steps)
    loop(3, 9, next_steps)
    loop(6, 9, lambda n: score(diagonal(n)))
    base = prior - 0.5 * (power[0:PD, :] + power[PD : 2 * PD, :])

    top = jnp.full((PD, KR), -jnp.inf, F32)
    for s in range(NS):
        value = acc[s * PD : (s + 1) * PD, :] + base
        acc[s * PD : (s + 1) * PD, :] = value
        top = jnp.maximum(top, value)
    top = jnp.max(top, axis=1, keepdims=True)
    total = jnp.zeros((PD, KR), F32)
    for s in range(NS):
        value = jnp.exp(acc[s * PD : (s + 1) * PD, :] - top)
        acc[s * PD : (s + 1) * PD, :] = value
        total = total + value
    total = jnp.sum(total, axis=1, keepdims=True)
    scale = 1.0 / total
    data_power = jnp.sum(dps[...], axis=1, keepdims=True)
    evidence = top + jnp.log(total) - 0.5 * data_power
    evidence = jnp.sum(evidence, axis=0, keepdims=True)
    scale2 = jnp.concatenate([scale, scale], axis=0)
    for s in range(NS // 2):
        w = acc[s * 128 : (s + 1) * 128, :] * scale2
        wt[:, s * 128 : (s + 1) * 128] = w.T.astype(BF)

    def block_at(i):
        return ahead((i + 1) % 16)

    def moment(i):
        b = block_at(i)
        part = dot_nn(wt[...], vv[:, lanes(b, 256)])
        sbuf[0] = part[:, :128]
        sbuf[1] = part[:, 128:]
        own_s[b] = sbuf[core]
        send_x[b] = sbuf[1 - core].astype(BF)
        send(send_x.at[b], recv_x.at[b], s_x, r_x.at[b], (z, mate))

    def pair_sum(i):
        b = block_at(i)
        wait(recv_x.at[b], r_x.at[b])
        return (own_s[b] + recv_x[b].astype(F32)).astype(BF), b

    def plane(i):
        value, b = pair_sum(i)
        d = (i + 1) % 16
        send_s[b] = value

        @pl.when(d // 4 > 0)
        def _():
            send(send_s.at[b, 0:HR], recv_s.at[0, cx, b % 4], s_s, r_s.at[0], (z, 2 * ((b // 4) * 4 + cy) + core))

        @pl.when(d // 4 == 0)
        def _():
            recv_s[0, cx, b % 4] = value[0:HR]

        @pl.when(d % 4 > 0)
        def _():
            send(send_s.at[b, HR:KR], recv_s.at[1, cy, b // 4], s_s, r_s.at[1], (z, 2 * (cx * 4 + b % 4) + core))

        @pl.when(d % 4 == 0)
        def _():
            recv_s[1, cy, b // 4] = value[HR:KR]

    loop(0, LAG, moment)

    def both_steps(i):
        moment(i)
        plane(i - LAG)

    loop(LAG, 16, both_steps)
    loop(16 - LAG, 16, plane)

    hot8 = jnp.concatenate([hot] * NS, axis=0)
    by_group = dot_nn(wt[...], hot8)
    groups = by_group[0:NZ]
    for r in range(1, R):
        groups = groups + by_group[r * NZ : (r + 1) * NZ]
    gw_high, gw_low = two_parts(groups)
    ev_high, ev_low = two_parts(evidence)
    for k in range(NZ):
        stage[k, R : R + 1, :] = gw_high[k : k + 1].astype(F32)
        stage[k, R + 1 : R + 2, :] = gw_low[k : k + 1].astype(F32)
        stage[k, R + 2 : R + 3, :] = jnp.broadcast_to(ev_high.astype(F32), (1, 128))
        stage[k, R + 3 : R + 4, :] = jnp.broadcast_to(ev_low.astype(F32), (1, 128))

    for half in range(2):
        wait(recv_s.at[half, pl.ds(0, 3)], r_s.at[half])
        here, source, step = (cy, cy, 1) if half == 0 else (cx, cx, 4)
        for n in range(4):
            to = (here + n) % 4
            part = recv_s[half, 0, to].astype(F32)
            for t in range(1, 4):
                part = part + recv_s[half, t, to].astype(F32)
            if n:
                send_b[half, n] = part.astype(BF)
                send(send_b.at[half, n], recv_b.at[half, source], s_b, r_b.at[half], (z, 2 * ahead(n * step) + core))
            else:
                recv_b[half, source] = part.astype(BF)
    for half in range(2):
        wait(recv_b.at[half, pl.ds(0, 3)], r_b.at[half])
        part = recv_b[half, 0].astype(F32)
        for t in range(1, 4):
            part = part + recv_b[half, t].astype(F32)
        ssum[half * HR : (half + 1) * HR, :] = part
    for k in range(NZ):
        stage[k, 0:R, :] = ssum[pl.ds(k, R, stride=NZ), :]
    send_3[...] = stage[...].astype(BF)

    def start_3(d):
        to = (z + d) % NZ
        send(send_3.at[to], recv_3.at[z], s_3, r_3, (to, g))

    loop(1, 16, start_3)
    recv_3[pl.ds(z, 1)] = send_3[pl.ds(z, 1)]
    wait(recv_3.at[pl.ds(0, 15)], r_3)
    last = recv_3[0].astype(F32)
    for t in range(1, NZ):
        last = last + recv_3[t].astype(F32)
    a16[...] = last
    for row in (R, R + 2):
        high, low = two_parts(last[row : row + 1] + last[row + 1 : row + 2])
        a16[row : row + 1, :] = high.astype(F32)
        a16[row + 1 : row + 2, :] = low.astype(F32)
    fin[pl.ds(g, 1)] = a16[...].astype(BF)[None]
    tile = fin.at[g]

    def start_5(d):
        for c in range(2):
            send(tile, tile, s_5, r_5, (z, 2 * ahead(d) + c))

    loop(1, 16, start_5)
    send(tile, tile, s_5, r_5, (z, mate))
    wait(fin.at[pl.ds(0, 31)], r_5)
    fin_out[...] = fin[...]

    wait(recv_a.at[pl.ds(0, 15)], s_a1)
    wait(a_all.at[:, pl.ds(0, 6 * 128)], s_a2)
    wait(a_all.at[0:HR, pl.ds(0, 18 * 128)], s_a2b)
    wait(a_all.at[:, pl.ds(0, HALF)], s_a3)
    wait(send_x, s_x)
    wait(recv_s.at[:, pl.ds(0, 3)], s_s)
    wait(send_b.at[:, pl.ds(0, 3)], s_b)
    wait(send_3.at[pl.ds(0, 15)], s_3)
    wait(fin.at[pl.ds(0, 31)], s_5)


def finish(fin, ctf, out, ctf_out, ev_out):
    rest = jnp.zeros((16 - R, 128), F32)
    for t in range(NC):
        for c in range(2):
            block = fin[2 * t + c].astype(F32)
            out[pl.ds(c * NC + t, R, stride=2 * NC), :] = block[0:R]
            rest = rest + block[R:16]
    groups = jnp.broadcast_to(rest[0:1] + rest[1:2], (G, 128)).T
    for t in range(HALF // 128):
        f = slice(t * 128, (t + 1) * 128)
        ctf_out[:, f] = jnp.sum(ctf[:, f] * ctf[:, f] * groups, axis=0, keepdims=True)
    ev_out[...] = (rest[2:3] + rest[3:4]) * (1.0 / (PD * NZ * NC * 2 * HALF))


def shards(dft, twiddle, particles, references, slot_class, log_prior, shift_offsets, group_ids, ctf_table, noise_power):
    vmem = pl.BlockSpec(memory_space=pltpu.VMEM)
    hbm = pl.BlockSpec(memory_space=pl.ANY)
    dma = pltpu.SemaphoreType.DMA
    tiles = pl.pallas_call(
        kernel,
        out_shape=jax.ShapeDtypeStruct((2 * NC, 16, 128), BF),
        in_specs=[hbm] * 10,
        out_specs=vmem,
        scratch_shapes=[
            pltpu.VMEM((1, R, FR), BF),
            pltpu.SMEM((NZ,), jnp.int32),
            pltpu.SMEM((NZ,), F32),
            pltpu.SMEM((2, NS), jnp.int32),
            pltpu.VMEM((1, PD), jnp.int32),
            pltpu.VMEM((1, HALF), F32),
            pltpu.VMEM((2, 8, 256), F32),
            pltpu.VMEM((PD, FR), BF),
            pltpu.VMEM((G, HALF), F32),
            pltpu.VMEM((2, 512, 512), BF),
            pltpu.VMEM((512, 512), BF),
            pltpu.VMEM((512, 512), F32),
            pltpu.VMEM((NS, HALF), F32),
            pltpu.VMEM((NS, HALF), F32),
            pltpu.VMEM((PD, HALF), F32),
            pltpu.VMEM((2 * PD, HALF), BF),
            pltpu.VMEM((NS * PD, FR), BF),
            pltpu.VMEM((PD, 128), F32),
            pltpu.VMEM((KR, FR), BF),
            pltpu.VMEM((2 * PD, KR), F32),
            pltpu.VMEM((NS * PD, KR), F32),
            pltpu.VMEM((KR, NS * PD), BF),
            pltpu.VMEM((16, 128), BF),
            pltpu.VMEM((16, 128), F32),
            pltpu.VMEM((NZ, 16, 128), BF),
            pltpu.VMEM((KR, 128), F32),
            pltpu.VMEM((2, KR, 128), F32),
            pltpu.VMEM((NC, KR, 128), F32),
            pltpu.VMEM((NC, KR, 128), BF),
            pltpu.VMEM((NC, KR, 128), BF),
            pltpu.VMEM((NC, KR, 128), BF),
            pltpu.VMEM((2, 4, 4, HR, 128), BF),
            pltpu.VMEM((2, 4, HR, 128), BF),
            pltpu.VMEM((2, 4, HR, 128), BF),
            pltpu.VMEM((KR, 128), F32),
            pltpu.VMEM((NZ, 16, 128), F32),
            pltpu.VMEM((NZ, 16, 128), BF),
            pltpu.VMEM((NZ, 16, 128), BF),
            pltpu.VMEM((2 * NC, 16, 128), BF),
            dma((10,)),
            dma, dma,
            dma, dma, dma((16,)), dma((16,)),
            dma, dma((16,)),
            dma, dma((16,)),
            dma, dma((2,)),
            dma, dma((2,)),
            dma, dma,
            dma, dma,
        ],
        compiler_params=pltpu.CompilerParams(
            collective_id=0, has_side_effects=True, vmem_limit_bytes=56 * 1024 * 1024
        ),
    )(
        particles, references, slot_class, log_prior, shift_offsets.T,
        group_ids.reshape(1, PD), ctf_table, noise_power.reshape(1, HALF), dft, twiddle,
    )
    class_sums, ctf_power, evidence = pl.pallas_call(
        finish,
        out_shape=(
            jax.ShapeDtypeStruct((R * FR // 128, 128), F32),
            jax.ShapeDtypeStruct((1, HALF), F32),
            jax.ShapeDtypeStruct((1, 128), F32),
        ),
        in_specs=[vmem, vmem],
        out_specs=(vmem, vmem, vmem),
    )(tiles, ctf_table)
    return class_sums.reshape(1, R, FR), ctf_power, evidence[0, 0]


def solution(mesh):
    dft, twiddle = dft_tables()
    split = ("gx", "gy")
    in_specs = (P(split, None), P("gx", None, None), P(), P(), P(), P(split), P(), P())
    out_specs = (P("gx", None, None), P("gx", None), P())

    def run(*args):
        body = functools.partial(shards, jnp.asarray(dft), jnp.asarray(twiddle))
        return jax.shard_map(body, mesh=mesh, in_specs=in_specs, out_specs=out_specs, check_vma=False)(*args)

    return run
```

```python
import functools

import jax
import jax.numpy as jnp
import ml_dtypes
import numpy as np
from jax import lax
from jax.experimental import pallas as pl
from jax.experimental.pallas import tpu as pltpu
from jax.sharding import PartitionSpec as P

L = 64
R = 12
NS = 8
G = 128
HALF = 2048
FR = 4096
PD = 64
NZ = 16
NC = 16
LAG = 8
HR = R * NZ // 2
KR = R * NZ
BF = jnp.bfloat16
F32 = jnp.float32
MESH = pl.DeviceIdType.MESH


def dft_tables():
    y2, x = np.divmod(np.arange(512), 64)
    low, v = np.divmod(np.arange(256), 32)
    turns = (8 * y2[:, None] * low[None] + x[:, None] * v[None]) % 64
    angle = turns * (2.0 * np.pi / 64)
    table = np.concatenate([np.cos(angle), -np.sin(angle)], axis=1) / 64
    high = table.astype(ml_dtypes.bfloat16)
    rest = (table - high.astype(np.float64)).astype(ml_dtypes.bfloat16)
    twist = (np.arange(8)[:, None] * low[None]) * (2.0 * np.pi / 64)
    twiddle = np.stack([np.cos(twist), -np.sin(twist)]).astype(np.float32)
    return np.stack([high, rest]), twiddle


def c_add(a, b):
    return a[0] + b[0], a[1] + b[1]


def c_sub(a, b):
    return a[0] - b[0], a[1] - b[1]


def c_mul(a, b):
    return a[0] * b[0] - a[1] * b[1], a[0] * b[1] + a[1] * b[0]


def minus_i(a):
    return a[1], -a[0]


def dft8(a):
    root = np.float32(np.sqrt(0.5))
    s = [c_add(a[n], a[n + 4]) for n in range(4)]
    d = [c_sub(a[n], a[n + 4]) for n in range(4)]
    even, odd = c_add(s[0], s[2]), c_add(s[1], s[3])
    x0, x4 = c_add(even, odd), c_sub(even, odd)
    even, odd = c_sub(s[0], s[2]), minus_i(c_sub(s[1], s[3]))
    x2, x6 = c_add(even, odd), c_sub(even, odd)
    w1 = [(root * (q[0] + q[1]), root * (q[1] - q[0])) for q in (d[1], d[3])]
    w3 = [(root * (q[1] - q[0]), -root * (q[0] + q[1])) for q in (d[1], d[3])]
    even, odd = c_add(d[0], minus_i(d[2])), c_add(w1[0], w3[1])
    x1, x5 = c_add(even, odd), c_sub(even, odd)
    even, odd = c_sub(d[0], minus_i(d[2])), c_add(w3[0], w1[1])
    x3, x7 = c_add(even, odd), c_sub(even, odd)
    return [x0, x1, x2, x3, x4, x5, x6, x7]


def two_parts(value):
    high = value.astype(BF)
    return high, (value - high.astype(F32)).astype(BF)


def dot_nt(a, b):
    return lax.dot_general(a, b, (((1,), (1,)), ((), ())), preferred_element_type=F32)


def dot_nn(a, b):
    return jnp.dot(a, b, preferred_element_type=F32)


def sine_of(turns):
    t = jnp.bitwise_and(turns, 63)
    half = jnp.bitwise_and(t, 31)
    quarter = jnp.minimum(half, 32 - half)
    a = quarter.astype(F32) * np.float32(np.pi / 32)
    q = a * a
    poly = np.float32(-2.5052108385441720e-08)
    for c in (2.7557319223985893e-06, -1.9841269841269841e-04, 8.3333333333333332e-03, -1.6666666666666666e-01):
        poly = poly * q + np.float32(c)
    value = a + a * (q * poly)
    return jnp.where(t >= 32, -value, value)


def kernel(
    part_hbm, refs_hbm, slot_hbm, prior_hbm, shifts_hbm, ids_hbm, ctf_hbm, noise_hbm, dft_hbm, twiddle_hbm,
    fin_out,
    refs, slot_class, log_prior, shifts, ids, noise, twiddle, pv, ctf, dft, pd, tt, cosb, sinb, wh, pw, vv, dps, a_all, power, acc, wt,
    send_a, a16, recv_a, a32, sbuf, own_s, send_x, recv_x, send_s, recv_s, send_b, recv_b,
    ssum, stage, send_3, recv_3, fin,
    load_sem, s_a1, r_a1, s_a2, s_a2b, r_a2, r_a2b, s_a3, r_a3, s_x, r_x, s_s, r_s, s_b, r_b, s_3, r_3, s_5, r_5,
):
    z = lax.axis_index("gx")
    g = lax.axis_index("gy")
    chip, core = g // 2, g % 2
    cx, cy = chip // 4, chip % 4
    mate = 2 * chip + 1 - core

    def ahead(d):
        return ((cx + d // 4) % 4) * 4 + (cy + d % 4) % 4

    def behind(d):
        return ((cx + 4 - d // 4) % 4) * 4 + (cy + 4 - d % 4) % 4

    def send(src, dst, s, r, to):
        pltpu.make_async_remote_copy(
            src_ref=src, dst_ref=dst, send_sem=s, recv_sem=r, device_id=to, device_id_type=MESH
        ).start()

    def wait(ref, sem):
        pltpu.make_async_copy(ref, ref, sem).wait()

    def loop(lo, hi, body):
        def step(i, carry):
            body(i)
            return carry

        lax.fori_loop(lo, hi, step, 0)

    def lanes(index, width=128):
        return pl.ds(pl.multiple_of(index * width, width), width)

    barrier = pltpu.get_barrier_semaphore()

    def greet_z(d):
        pl.semaphore_signal(barrier, inc=1, device_id=((z + d) % NZ, g), device_id_type=MESH)

    def greet_plane(d):
        pl.semaphore_signal(barrier, inc=1, device_id=(z, 2 * ahead(d)), device_id_type=MESH)
        pl.semaphore_signal(barrier, inc=1, device_id=(z, 2 * ahead(d) + 1), device_id_type=MESH)

    loop(1, 16, greet_z)
    loads = [
        pltpu.make_async_copy(src, dst, load_sem.at[n])
        for n, (src, dst) in enumerate(
            (
                (refs_hbm, refs), (shifts_hbm, shifts), (ids_hbm, ids), (noise_hbm, noise), (ctf_hbm, ctf),
                (part_hbm, pv), (dft_hbm, dft), (twiddle_hbm, twiddle), (slot_hbm, slot_class), (prior_hbm, log_prior),
            )
        )
    ]
    for load in loads:
        load.start()
    loop(1, 16, greet_plane)
    pl.semaphore_signal(barrier, inc=1, device_id=(z, mate), device_id_type=MESH)
    for load in loads[:4]:
        load.wait()

    a16[...] = jnp.zeros((16, 128), F32)
    a16[0:R, :] = refs[0, :, lanes(core * 16 + chip)].astype(F32)
    send_a[...] = a16[...].astype(BF)
    freq = lax.broadcasted_iota(jnp.int32, (NS, HALF), 1)
    which = lax.broadcasted_iota(jnp.int32, (NS, 128), 0)
    down, along = jnp.zeros((NS, 128), jnp.int32), jnp.zeros((NS, 128), jnp.int32)
    for s in range(NS):
        down = jnp.where(which == s, shifts[0, s], down)
        along = jnp.where(which == s, shifts[1, s], along)
    turns = (freq // 32) * down[:, 0:1] + (freq % 32) * along[:, 0:1]
    cosb[...] = sine_of(turns + 16)
    sinb[...] = sine_of(turns)
    inv_noise = 1.0 / noise[...]
    hot_t = (lax.broadcasted_iota(jnp.int32, (G, PD), 0) == ids[...]).astype(F32)
    hot = hot_t.T.astype(BF)
    loads[4].wait()
    table_high, table_low = two_parts(ctf[...])
    rows = dot_nn(hot, table_high) + dot_nn(hot, table_low)
    wh[...] = rows * inv_noise
    power_high, power_low = two_parts(rows * rows * inv_noise)
    for t in range(NC):
        f = slice(t * 128, (t + 1) * 128)
        pw[:, t * 384 : (t + 1) * 384] = jnp.concatenate([power_high[:, f], power_low[:, f], power_high[:, f]], axis=1)

    pl.semaphore_wait(barrier, 46)

    def start_a1(d):
        to = (z + d) % NZ
        send(send_a, recv_a.at[z], s_a1, r_a1, (to, g))

    loop(1, 16, start_a1)
    recv_a[pl.ds(z, 1)] = send_a[...][None]

    lane = lax.broadcasted_iota(jnp.int32, (PD, 128), 1)
    loads[5].wait()
    for q in range(4):
        for r in range(4):
            a = pv[:, (q + 8 * r) * 128 : (q + 8 * r + 1) * 128].astype(F32)
            b = pv[:, (q + 8 * r + 4) * 128 : (q + 8 * r + 5) * 128].astype(F32)
            first = jnp.where(lane < 64, a, pltpu.roll(b, 64, 1))
            second = jnp.where(lane < 64, pltpu.roll(a, 64, 1), b)
            cols = slice(r * 128, (r + 1) * 128)
            pd[2 * q * PD : (2 * q + 1) * PD, cols] = first.astype(BF)
            pd[(2 * q + 1) * PD : (2 * q + 2) * PD, cols] = second.astype(BF)
    loads[6].wait()
    loads[7].wait()
    tt[...] = dot_nn(pd[...], dft[0]) + dot_nn(pd[...], dft[1])

    def spectrum(pb):
        at = pl.multiple_of(pb * 16, 16)
        total = jnp.zeros((16, 128), F32)
        for h in range(2):
            cols = slice(h * 128, (h + 1) * 128)
            terms = []
            for y1 in range(8):
                where = pl.ds(pl.multiple_of(y1 * PD + at, 16), 16)
                t = tt[where, h * 128 : h * 128 + 128], tt[where, 256 + h * 128 : 256 + h * 128 + 128]
                if y1:
                    t = c_mul(t, (twiddle[0, y1 : y1 + 1, cols], twiddle[1, y1 : y1 + 1, cols]))
                terms.append(t)
            for m, (re, im) in enumerate(dft8(terms)):
                block = 2 * m + h
                f = slice(block * 128, block * 128 + 128)
                total = total + (re * re + im * im) * (1.0 / noise[:, f])
                factor = wh[pl.ds(at, 16), f]
                re, im = re * factor, im * factor
                for s in range(NS):
                    c, n = cosb[s : s + 1, f], sinb[s : s + 1, f]
                    where = pl.ds(pl.multiple_of(s * PD + at, 16), 16)
                    vv[where, block * 256 : block * 256 + 128] = (re * c - im * n).astype(BF)
                    vv[where, block * 256 + 128 : block * 256 + 256] = (re * n + im * c).astype(BF)
        dps[pl.ds(at, 16), :] = total

    loop(0, 4, spectrum)

    loads[8].wait()
    loads[9].wait()
    slot = lax.broadcasted_iota(jnp.int32, (1, KR), 1) % NZ
    prior = jnp.zeros((1, KR), F32)
    for k in range(NZ):
        prior = jnp.where(slot == k, log_prior[slot_class[k]], prior)

    wait(recv_a.at[pl.ds(0, 15)], r_a1)
    for k in range(NZ):
        a32[pl.ds(k, R, stride=NZ), :] = recv_a[k].astype(F32)[0:R]
    a_all[:, lanes(g)] = a32[...].astype(BF)
    mine = a_all.at[:, lanes(g)]

    def start_a2(d):
        send(mine, mine, s_a2, r_a2.at[4 * d], (z, 2 * ahead(4 * d) + core))
        send(mine, mine, s_a2, r_a2.at[d], (z, 2 * ahead(d) + core))

    loop(1, 4, start_a2)
    send(mine, mine, s_a3, r_a3.at[0], (z, mate))

    acc[...] = jnp.zeros((NS * PD, KR), F32)
    power[...] = jnp.zeros((PD, KR), F32)

    def hand_on(block, d):
        send(block, block, s_a3, r_a3.at[d], (z, mate))

    def direct(i):
        for d, rows, first, step in ((4 * i, slice(0, HR), 4 * i, 1), (i, slice(HR, KR), i, 4)):
            at = lanes(2 * behind(d) + core)
            block = a_all.at[:, at]
            wait(block, r_a2.at[d])
            part = a_all.at[rows, at]
            for n in range(1, 4):
                sem = (r_a2 if step == 1 else r_a2b).at[first + n * step]
                send(part, part, s_a2b, sem, (z, 2 * ahead(n * step) + core))
            hand_on(block, d)

    def diagonal(n):
        return (n // 3 + 1) * 4 + n % 3 + 1

    def relayed(n):
        d = diagonal(n)
        at = lanes(2 * behind(d) + core)
        wait(a_all.at[0:HR, at], r_a2.at[d])
        wait(a_all.at[HR:KR, at], r_a2b.at[d])
        hand_on(a_all.at[:, at], d)

    def score(*offsets):
        pairs, sides, values, powers = [], [], [], []
        for d in offsets:
            b = behind(d)
            wait(a_all.at[:, lanes(2 * b + 1 - core)], r_a3.at[d])
            both = a_all[:, lanes(b, 256)]
            pairs.append(both)
            sides.append(vv[:, lanes(b, 256)])
            re, im = both[:, :128].astype(F32), both[:, 128:].astype(F32)
            high, low = two_parts(re * re + im * im)
            values.extend([high, high, low])
            powers.append(pw[:, lanes(b, 384)])
        acc[...] += dot_nt(jnp.concatenate(sides, axis=1), jnp.concatenate(pairs, axis=1))
        power[...] += dot_nt(jnp.concatenate(powers, axis=1), jnp.concatenate(values, axis=1))

    def first_steps(n):
        relayed(n)
        score(4 * (n + 1), n + 1)

    loop(1, 4, direct)
    loop(0, 3, first_steps)
    loop(3, 5, relayed)
    score(0, diagonal(0))
    for n in range(2):
        relayed(2 * n + 5)
        relayed(2 * n + 6)
        score(diagonal(2 * n + 1), diagonal(2 * n + 2))
    for n in range(2, 4):
        score(diagonal(2 * n + 1), diagonal(2 * n + 2))
    base = prior - 0.5 * power[...]

    top = jnp.full((PD, KR), -jnp.inf, F32)
    for s in range(NS):
        value = acc[s * PD : (s + 1) * PD, :] + base
        acc[s * PD : (s + 1) * PD, :] = value
        top = jnp.maximum(top, value)
    top = jnp.max(top, axis=1, keepdims=True)
    total = jnp.zeros((PD, KR), F32)
    for s in range(NS):
        value = jnp.exp(acc[s * PD : (s + 1) * PD, :] - top)
        acc[s * PD : (s + 1) * PD, :] = value
        total = total + value
    total = jnp.sum(total, axis=1, keepdims=True)
    scale = 1.0 / total
    data_power = jnp.sum(dps[...], axis=1, keepdims=True)
    evidence = top + jnp.log(total) - 0.5 * data_power
    evidence = jnp.sum(evidence, axis=0, keepdims=True)
    scale2 = jnp.concatenate([scale, scale], axis=0)
    for s in range(NS // 2):
        w = acc[s * 128 : (s + 1) * 128, :] * scale2
        wt[:, s * 128 : (s + 1) * 128] = w.T.astype(BF)

    def block_at(i):
        return ahead(5 * (i + 1) % 16)

    def moment(i):
        b = block_at(i)
        part = dot_nn(wt[...], vv[:, lanes(b, 256)])
        sbuf[0] = part[:, :128]
        sbuf[1] = part[:, 128:]
        own_s[b] = sbuf[core]
        send_x[b] = sbuf[1 - core].astype(BF)
        send(send_x.at[b], recv_x.at[b], s_x, r_x.at[b], (z, mate))

    def pair_sum(i):
        b = block_at(i)
        wait(recv_x.at[b], r_x.at[b])
        return (own_s[b] + recv_x[b].astype(F32)).astype(BF), b

    def plane(i):
        value, b = pair_sum(i)
        d = 5 * (i + 1) % 16
        send_s[b] = value

        @pl.when(d // 4 > 0)
        def _():
            send(send_s.at[b, 0:HR], recv_s.at[0, cx, b % 4], s_s, r_s.at[0], (z, 2 * ((b // 4) * 4 + cy) + core))

        @pl.when(d // 4 == 0)
        def _():
            recv_s[0, cx, b % 4] = value[0:HR]

        @pl.when(d % 4 > 0)
        def _():
            send(send_s.at[b, HR:KR], recv_s.at[1, cy, b // 4], s_s, r_s.at[1], (z, 2 * (cx * 4 + b % 4) + core))

        @pl.when(d % 4 == 0)
        def _():
            recv_s[1, cy, b // 4] = value[HR:KR]

    loop(0, LAG, moment)

    def both_steps(i):
        moment(i)
        plane(i - LAG)

    loop(LAG, 16, both_steps)
    loop(16 - LAG, 16, plane)

    hot8 = jnp.concatenate([hot] * NS, axis=0)
    by_group = dot_nn(wt[...], hot8)
    groups = by_group[0:NZ]
    for r in range(1, R):
        groups = groups + by_group[r * NZ : (r + 1) * NZ]
    gw_high, gw_low = two_parts(groups)
    ev_high, ev_low = two_parts(evidence)
    for k in range(NZ):
        stage[k, R : R + 1, :] = gw_high[k : k + 1].astype(F32)
        stage[k, R + 1 : R + 2, :] = gw_low[k : k + 1].astype(F32)
        stage[k, R + 2 : R + 3, :] = jnp.broadcast_to(ev_high.astype(F32), (1, 128))
        stage[k, R + 3 : R + 4, :] = jnp.broadcast_to(ev_low.astype(F32), (1, 128))

    for half in range(2):
        wait(recv_s.at[half, pl.ds(0, 3)], r_s.at[half])
        here, source, step = (cy, cy, 1) if half == 0 else (cx, cx, 4)
        for n in range(4):
            to = (here + n) % 4
            part = recv_s[half, 0, to].astype(F32)
            for t in range(1, 4):
                part = part + recv_s[half, t, to].astype(F32)
            if n:
                send_b[half, n] = part.astype(BF)
                send(send_b.at[half, n], recv_b.at[half, source], s_b, r_b.at[half], (z, 2 * ahead(n * step) + core))
            else:
                recv_b[half, source] = part.astype(BF)
    for half in range(2):
        wait(recv_b.at[half, pl.ds(0, 3)], r_b.at[half])
        part = recv_b[half, 0].astype(F32)
        for t in range(1, 4):
            part = part + recv_b[half, t].astype(F32)
        ssum[half * HR : (half + 1) * HR, :] = part
    for k in range(NZ):
        stage[k, 0:R, :] = ssum[pl.ds(k, R, stride=NZ), :]
    send_3[...] = stage[...].astype(BF)

    def start_3(d):
        to = (z + d) % NZ
        send(send_3.at[to], recv_3.at[z], s_3, r_3, (to, g))

    loop(1, 16, start_3)
    recv_3[pl.ds(z, 1)] = send_3[pl.ds(z, 1)]
    wait(recv_3.at[pl.ds(0, 15)], r_3)
    last = recv_3[0].astype(F32)
    for t in range(1, NZ):
        last = last + recv_3[t].astype(F32)
    a16[...] = last
    for row in (R, R + 2):
        high, low = two_parts(last[row : row + 1] + last[row + 1 : row + 2])
        a16[row : row + 1, :] = high.astype(F32)
        a16[row + 1 : row + 2, :] = low.astype(F32)
    fin[pl.ds(g, 1)] = a16[...].astype(BF)[None]
    tile = fin.at[g]

    def start_5(d):
        for c in range(2):
            send(tile, tile, s_5, r_5, (z, 2 * ahead(d) + c))

    loop(1, 16, start_5)
    send(tile, tile, s_5, r_5, (z, mate))
    wait(fin.at[pl.ds(0, 31)], r_5)
    fin_out[...] = fin[...]

    wait(recv_a.at[pl.ds(0, 15)], s_a1)
    wait(a_all.at[:, pl.ds(0, 6 * 128)], s_a2)
    wait(a_all.at[0:HR, pl.ds(0, 18 * 128)], s_a2b)
    wait(a_all.at[:, pl.ds(0, HALF)], s_a3)
    wait(send_x, s_x)
    wait(recv_s.at[:, pl.ds(0, 3)], s_s)
    wait(send_b.at[:, pl.ds(0, 3)], s_b)
    wait(send_3.at[pl.ds(0, 15)], s_3)
    wait(fin.at[pl.ds(0, 31)], s_5)


def finish(fin, ctf, out, ctf_out, ev_out):
    rest = jnp.zeros((16 - R, 128), F32)
    for t in range(NC):
        for c in range(2):
            block = fin[2 * t + c].astype(F32)
            out[pl.ds(c * NC + t, R, stride=2 * NC), :] = block[0:R]
            rest = rest + block[R:16]
    groups = jnp.broadcast_to(rest[0:1] + rest[1:2], (G, 128)).T
    for t in range(HALF // 128):
        f = slice(t * 128, (t + 1) * 128)
        ctf_out[:, f] = jnp.sum(ctf[:, f] * ctf[:, f] * groups, axis=0, keepdims=True)
    ev_out[...] = (rest[2:3] + rest[3:4]) * (1.0 / (PD * NZ * NC * 2 * HALF))


def shards(dft, twiddle, particles, references, slot_class, log_prior, shift_offsets, group_ids, ctf_table, noise_power):
    vmem = pl.BlockSpec(memory_space=pltpu.VMEM)
    hbm = pl.BlockSpec(memory_space=pl.ANY)
    dma = pltpu.SemaphoreType.DMA
    tiles = pl.pallas_call(
        kernel,
        out_shape=jax.ShapeDtypeStruct((2 * NC, 16, 128), BF),
        in_specs=[hbm] * 10,
        out_specs=vmem,
        scratch_shapes=[
            pltpu.VMEM((1, R, FR), BF),
            pltpu.SMEM((NZ,), jnp.int32),
            pltpu.SMEM((NZ,), F32),
            pltpu.SMEM((2, NS), jnp.int32),
            pltpu.VMEM((1, PD), jnp.int32),
            pltpu.VMEM((1, HALF), F32),
            pltpu.VMEM((2, 8, 256), F32),
            pltpu.VMEM((PD, FR), BF),
            pltpu.VMEM((G, HALF), F32),
            pltpu.VMEM((2, 512, 512), BF),
            pltpu.VMEM((512, 512), BF),
            pltpu.VMEM((512, 512), F32),
            pltpu.VMEM((NS, HALF), F32),
            pltpu.VMEM((NS, HALF), F32),
            pltpu.VMEM((PD, HALF), F32),
            pltpu.VMEM((PD, NC * 384), BF),
            pltpu.VMEM((NS * PD, FR), BF),
            pltpu.VMEM((PD, 128), F32),
            pltpu.VMEM((KR, FR), BF),
            pltpu.VMEM((PD, KR), F32),
            pltpu.VMEM((NS * PD, KR), F32),
            pltpu.VMEM((KR, NS * PD), BF),
            pltpu.VMEM((16, 128), BF),
            pltpu.VMEM((16, 128), F32),
            pltpu.VMEM((NZ, 16, 128), BF),
            pltpu.VMEM((KR, 128), F32),
            pltpu.VMEM((2, KR, 128), F32),
            pltpu.VMEM((NC, KR, 128), F32),
            pltpu.VMEM((NC, KR, 128), BF),
            pltpu.VMEM((NC, KR, 128), BF),
            pltpu.VMEM((NC, KR, 128), BF),
            pltpu.VMEM((2, 4, 4, HR, 128), BF),
            pltpu.VMEM((2, 4, HR, 128), BF),
            pltpu.VMEM((2, 4, HR, 128), BF),
            pltpu.VMEM((KR, 128), F32),
            pltpu.VMEM((NZ, 16, 128), F32),
            pltpu.VMEM((NZ, 16, 128), BF),
            pltpu.VMEM((NZ, 16, 128), BF),
            pltpu.VMEM((2 * NC, 16, 128), BF),
            dma((10,)),
            dma, dma,
            dma, dma, dma((16,)), dma((16,)),
            dma, dma((16,)),
            dma, dma((16,)),
            dma, dma((2,)),
            dma, dma((2,)),
            dma, dma,
            dma, dma,
        ],
        compiler_params=pltpu.CompilerParams(
            collective_id=0, has_side_effects=True, vmem_limit_bytes=56 * 1024 * 1024
        ),
    )(
        particles, references, slot_class, log_prior, shift_offsets.T,
        group_ids.reshape(1, PD), ctf_table, noise_power.reshape(1, HALF), dft, twiddle,
    )
    class_sums, ctf_power, evidence = pl.pallas_call(
        finish,
        out_shape=(
            jax.ShapeDtypeStruct((R * FR // 128, 128), F32),
            jax.ShapeDtypeStruct((1, HALF), F32),
            jax.ShapeDtypeStruct((1, 128), F32),
        ),
        in_specs=[vmem, vmem],
        out_specs=(vmem, vmem, vmem),
    )(tiles, ctf_table)
    return class_sums.reshape(1, R, FR), ctf_power, evidence[0, 0]


def solution(mesh):
    dft, twiddle = dft_tables()
    split = ("gx", "gy")
    in_specs = (P(split, None), P("gx", None, None), P(), P(), P(), P(split), P(), P())
    out_specs = (P("gx", None, None), P("gx", None), P())

    def run(*args):
        body = functools.partial(shards, jnp.asarray(dft), jnp.asarray(twiddle))
        return jax.shard_map(body, mesh=mesh, in_specs=in_specs, out_specs=out_specs, check_vma=False)(*args)

    return run
```

```python
import functools

import jax
import jax.numpy as jnp
import ml_dtypes
import numpy as np
from jax import lax
from jax.experimental import pallas as pl
from jax.experimental.pallas import tpu as pltpu
from jax.sharding import PartitionSpec as P

L = 64
R = 12
NS = 8
G = 128
HALF = 2048
FR = 4096
PD = 64
NZ = 16
NC = 16
LAG = 8
RING_ORDER = (8, 7, 9, 6, 10, 5, 11, 4, 12, 3, 13, 2, 14, 1, 15)
PLANE_ORDER = (10, 6, 9, 11, 14, 2, 8, 5, 7, 13, 15, 1, 3, 4, 12)
HR = R * NZ // 2
KR = R * NZ
BF = jnp.bfloat16
F32 = jnp.float32
MESH = pl.DeviceIdType.MESH


def dft_tables():
    y2, x = np.divmod(np.arange(512), 64)
    low, v = np.divmod(np.arange(256), 32)
    turns = (8 * y2[:, None] * low[None] + x[:, None] * v[None]) % 64
    angle = turns * (2.0 * np.pi / 64)
    table = np.concatenate([np.cos(angle), -np.sin(angle)], axis=1) / 64
    high = table.astype(ml_dtypes.bfloat16)
    rest = (table - high.astype(np.float64)).astype(ml_dtypes.bfloat16)
    twist = (np.arange(8)[:, None] * low[None]) * (2.0 * np.pi / 64)
    twiddle = np.stack([np.cos(twist), -np.sin(twist)]).astype(np.float32)
    return np.stack([high, rest]), twiddle


def c_add(a, b):
    return a[0] + b[0], a[1] + b[1]


def c_sub(a, b):
    return a[0] - b[0], a[1] - b[1]


def c_mul(a, b):
    return a[0] * b[0] - a[1] * b[1], a[0] * b[1] + a[1] * b[0]


def minus_i(a):
    return a[1], -a[0]


def dft8(a):
    root = np.float32(np.sqrt(0.5))
    s = [c_add(a[n], a[n + 4]) for n in range(4)]
    d = [c_sub(a[n], a[n + 4]) for n in range(4)]
    even, odd = c_add(s[0], s[2]), c_add(s[1], s[3])
    x0, x4 = c_add(even, odd), c_sub(even, odd)
    even, odd = c_sub(s[0], s[2]), minus_i(c_sub(s[1], s[3]))
    x2, x6 = c_add(even, odd), c_sub(even, odd)
    w1 = [(root * (q[0] + q[1]), root * (q[1] - q[0])) for q in (d[1], d[3])]
    w3 = [(root * (q[1] - q[0]), -root * (q[0] + q[1])) for q in (d[1], d[3])]
    even, odd = c_add(d[0], minus_i(d[2])), c_add(w1[0], w3[1])
    x1, x5 = c_add(even, odd), c_sub(even, odd)
    even, odd = c_sub(d[0], minus_i(d[2])), c_add(w3[0], w1[1])
    x3, x7 = c_add(even, odd), c_sub(even, odd)
    return [x0, x1, x2, x3, x4, x5, x6, x7]


def two_parts(value):
    high = value.astype(BF)
    return high, (value - high.astype(F32)).astype(BF)


def dot_nt(a, b):
    return lax.dot_general(a, b, (((1,), (1,)), ((), ())), preferred_element_type=F32)


def dot_nn(a, b):
    return jnp.dot(a, b, preferred_element_type=F32)


def sine_of(turns):
    t = jnp.bitwise_and(turns, 63)
    half = jnp.bitwise_and(t, 31)
    quarter = jnp.minimum(half, 32 - half)
    a = quarter.astype(F32) * np.float32(np.pi / 32)
    q = a * a
    poly = np.float32(-2.5052108385441720e-08)
    for c in (2.7557319223985893e-06, -1.9841269841269841e-04, 8.3333333333333332e-03, -1.6666666666666666e-01):
        poly = poly * q + np.float32(c)
    value = a + a * (q * poly)
    return jnp.where(t >= 32, -value, value)


def kernel(
    part_hbm, refs_hbm, slot_hbm, prior_hbm, shifts_hbm, ids_hbm, ctf_hbm, noise_hbm, dft_hbm, twiddle_hbm,
    fin_out,
    refs, slot_class, log_prior, shifts, ids, noise, twiddle, pv, ctf, dft, pd, tt, cosb, sinb, wh, pw, vv, dps, a_all, power, acc, wt,
    send_a, a16, recv_a, a32, sbuf, own_s, send_x, recv_x, send_s, recv_s, send_b, recv_b,
    ssum, stage, send_3, recv_3, fin,
    load_sem, s_a1, r_a1, s_a2, s_a2b, r_a2, r_a2b, s_a3, r_a3, s_x, r_x, s_s, r_s, s_b, r_b, s_3, r_3, s_5, r_5,
):
    z = lax.axis_index("gx")
    g = lax.axis_index("gy")
    chip, core = g // 2, g % 2
    cx, cy = chip // 4, chip % 4
    mate = 2 * chip + 1 - core

    def ahead(d):
        return ((cx + d // 4) % 4) * 4 + (cy + d % 4) % 4

    def behind(d):
        return ((cx + 4 - d // 4) % 4) * 4 + (cy + 4 - d % 4) % 4

    def send(src, dst, s, r, to):
        pltpu.make_async_remote_copy(
            src_ref=src, dst_ref=dst, send_sem=s, recv_sem=r, device_id=to, device_id_type=MESH
        ).start()

    def wait(ref, sem):
        pltpu.make_async_copy(ref, ref, sem).wait()

    def loop(lo, hi, body):
        def step(i, carry):
            body(i)
            return carry

        lax.fori_loop(lo, hi, step, 0)

    def lanes(index, width=128):
        return pl.ds(pl.multiple_of(index * width, width), width)

    barrier = pltpu.get_barrier_semaphore()

    def greet_z(d):
        pl.semaphore_signal(barrier, inc=1, device_id=((z + d) % NZ, g), device_id_type=MESH)

    def greet_plane(d):
        pl.semaphore_signal(barrier, inc=1, device_id=(z, 2 * ahead(d)), device_id_type=MESH)
        pl.semaphore_signal(barrier, inc=1, device_id=(z, 2 * ahead(d) + 1), device_id_type=MESH)

    loop(1, 16, greet_z)
    loads = [
        pltpu.make_async_copy(src, dst, load_sem.at[n])
        for n, (src, dst) in enumerate(
            (
                (refs_hbm, refs), (shifts_hbm, shifts), (ids_hbm, ids), (noise_hbm, noise), (ctf_hbm, ctf),
                (part_hbm, pv), (dft_hbm, dft), (twiddle_hbm, twiddle), (slot_hbm, slot_class), (prior_hbm, log_prior),
            )
        )
    ]
    for load in loads:
        load.start()
    loop(1, 16, greet_plane)
    pl.semaphore_signal(barrier, inc=1, device_id=(z, mate), device_id_type=MESH)
    for load in loads[:4]:
        load.wait()

    a16[...] = jnp.zeros((16, 128), F32)
    a16[0:R, :] = refs[0, :, lanes(core * 16 + chip)].astype(F32)
    send_a[...] = a16[...].astype(BF)
    freq = lax.broadcasted_iota(jnp.int32, (NS, HALF), 1)
    which = lax.broadcasted_iota(jnp.int32, (NS, 128), 0)
    down, along = jnp.zeros((NS, 128), jnp.int32), jnp.zeros((NS, 128), jnp.int32)
    for s in range(NS):
        down = jnp.where(which == s, shifts[0, s], down)
        along = jnp.where(which == s, shifts[1, s], along)
    turns = (freq // 32) * down[:, 0:1] + (freq % 32) * along[:, 0:1]
    cosb[...] = sine_of(turns + 16)
    sinb[...] = sine_of(turns)
    inv_noise = 1.0 / noise[...]
    hot_t = (lax.broadcasted_iota(jnp.int32, (G, PD), 0) == ids[...]).astype(F32)
    hot = hot_t.T.astype(BF)
    loads[4].wait()
    table_high, table_low = two_parts(ctf[...])
    rows = dot_nn(hot, table_high) + dot_nn(hot, table_low)
    wh[...] = rows * inv_noise
    power_high, power_low = two_parts(rows * rows * inv_noise)
    for t in range(NC):
        f = slice(t * 128, (t + 1) * 128)
        pw[:, t * 384 : (t + 1) * 384] = jnp.concatenate([power_high[:, f], power_low[:, f], power_high[:, f]], axis=1)

    pl.semaphore_wait(barrier, 46)

    def start_a1(d):
        to = (z + d) % NZ
        send(send_a, recv_a.at[z], s_a1, r_a1, (to, g))

    for d in RING_ORDER:
        start_a1(d)
    recv_a[pl.ds(z, 1)] = send_a[...][None]

    lane = lax.broadcasted_iota(jnp.int32, (PD, 128), 1)
    loads[5].wait()
    for q in range(4):
        for r in range(4):
            a = pv[:, (q + 8 * r) * 128 : (q + 8 * r + 1) * 128].astype(F32)
            b = pv[:, (q + 8 * r + 4) * 128 : (q + 8 * r + 5) * 128].astype(F32)
            first = jnp.where(lane < 64, a, pltpu.roll(b, 64, 1))
            second = jnp.where(lane < 64, pltpu.roll(a, 64, 1), b)
            cols = slice(r * 128, (r + 1) * 128)
            pd[2 * q * PD : (2 * q + 1) * PD, cols] = first.astype(BF)
            pd[(2 * q + 1) * PD : (2 * q + 2) * PD, cols] = second.astype(BF)
    loads[6].wait()
    loads[7].wait()
    tt[...] = dot_nn(pd[...], dft[0]) + dot_nn(pd[...], dft[1])

    def spectrum(pb):
        at = pl.multiple_of(pb * 16, 16)
        total = jnp.zeros((16, 128), F32)
        for h in range(2):
            cols = slice(h * 128, (h + 1) * 128)
            terms = []
            for y1 in range(8):
                where = pl.ds(pl.multiple_of(y1 * PD + at, 16), 16)
                t = tt[where, h * 128 : h * 128 + 128], tt[where, 256 + h * 128 : 256 + h * 128 + 128]
                if y1:
                    t = c_mul(t, (twiddle[0, y1 : y1 + 1, cols], twiddle[1, y1 : y1 + 1, cols]))
                terms.append(t)
            for m, (re, im) in enumerate(dft8(terms)):
                block = 2 * m + h
                f = slice(block * 128, block * 128 + 128)
                total = total + (re * re + im * im) * (1.0 / noise[:, f])
                factor = wh[pl.ds(at, 16), f]
                re, im = re * factor, im * factor
                for s in range(NS):
                    c, n = cosb[s : s + 1, f], sinb[s : s + 1, f]
                    where = pl.ds(pl.multiple_of(s * PD + at, 16), 16)
                    vv[where, block * 256 : block * 256 + 128] = (re * c - im * n).astype(BF)
                    vv[where, block * 256 + 128 : block * 256 + 256] = (re * n + im * c).astype(BF)
        dps[pl.ds(at, 16), :] = total

    loop(0, 4, spectrum)

    loads[8].wait()
    loads[9].wait()
    slot = lax.broadcasted_iota(jnp.int32, (1, KR), 1) % NZ
    prior = jnp.zeros((1, KR), F32)
    for k in range(NZ):
        prior = jnp.where(slot == k, log_prior[slot_class[k]], prior)

    wait(recv_a.at[pl.ds(0, 15)], r_a1)
    for k in range(NZ):
        a32[pl.ds(k, R, stride=NZ), :] = recv_a[k].astype(F32)[0:R]
    a_all[:, lanes(g)] = a32[...].astype(BF)
    mine = a_all.at[:, lanes(g)]

    def start_a2(d):
        send(mine, mine, s_a2, r_a2.at[4 * d], (z, 2 * ahead(4 * d) + core))
        send(mine, mine, s_a2, r_a2.at[d], (z, 2 * ahead(d) + core))

    loop(1, 4, start_a2)
    send(mine, mine, s_a3, r_a3.at[0], (z, mate))

    acc[...] = jnp.zeros((NS * PD, KR), F32)
    power[...] = jnp.zeros((PD, KR), F32)

    def hand_on(block, d):
        send(block, block, s_a3, r_a3.at[d], (z, mate))

    def direct(i):
        for d, rows, first, step in ((4 * i, slice(0, HR), 4 * i, 1), (i, slice(HR, KR), i, 4)):
            at = lanes(2 * behind(d) + core)
            block = a_all.at[:, at]
            wait(block, r_a2.at[d])
            part = a_all.at[rows, at]
            for n in range(1, 4):
                sem = (r_a2 if step == 1 else r_a2b).at[first + n * step]
                send(part, part, s_a2b, sem, (z, 2 * ahead(n * step) + core))
            hand_on(block, d)

    def diagonal(n):
        return (n // 3 + 1) * 4 + n % 3 + 1

    def relayed(n):
        d = diagonal(n)
        at = lanes(2 * behind(d) + core)
        wait(a_all.at[0:HR, at], r_a2.at[d])
        wait(a_all.at[HR:KR, at], r_a2b.at[d])
        hand_on(a_all.at[:, at], d)

    def score(*offsets):
        pairs, sides, values, powers = [], [], [], []
        for d in offsets:
            b = behind(d)
            wait(a_all.at[:, lanes(2 * b + 1 - core)], r_a3.at[d])
            both = a_all[:, lanes(b, 256)]
            pairs.append(both)
            sides.append(vv[:, lanes(b, 256)])
            re, im = both[:, :128].astype(F32), both[:, 128:].astype(F32)
            high, low = two_parts(re * re + im * im)
            values.extend([high, high, low])
            powers.append(pw[:, lanes(b, 384)])
        acc[...] += dot_nt(jnp.concatenate(sides, axis=1), jnp.concatenate(pairs, axis=1))
        power[...] += dot_nt(jnp.concatenate(powers, axis=1), jnp.concatenate(values, axis=1))

    def first_steps(n):
        relayed(n)
        score(4 * (n + 1), n + 1)

    loop(1, 4, direct)
    loop(0, 3, first_steps)
    loop(3, 5, relayed)
    score(0, diagonal(0))
    for n in range(2):
        relayed(2 * n + 5)
        relayed(2 * n + 6)
        score(diagonal(2 * n + 1), diagonal(2 * n + 2))
    for n in range(2, 4):
        score(diagonal(2 * n + 1), diagonal(2 * n + 2))
    base = prior - 0.5 * power[...]

    top = jnp.full((PD, KR), -jnp.inf, F32)
    for s in range(NS):
        value = acc[s * PD : (s + 1) * PD, :] + base
        acc[s * PD : (s + 1) * PD, :] = value
        top = jnp.maximum(top, value)
    top = jnp.max(top, axis=1, keepdims=True)
    total = jnp.zeros((PD, KR), F32)
    for s in range(NS):
        value = jnp.exp(acc[s * PD : (s + 1) * PD, :] - top)
        acc[s * PD : (s + 1) * PD, :] = value
        total = total + value
    total = jnp.sum(total, axis=1, keepdims=True)
    scale = 1.0 / total
    data_power = jnp.sum(dps[...], axis=1, keepdims=True)
    evidence = top + jnp.log(total) - 0.5 * data_power
    evidence = jnp.sum(evidence, axis=0, keepdims=True)
    scale2 = jnp.concatenate([scale, scale], axis=0)
    for s in range(NS // 2):
        w = acc[s * 128 : (s + 1) * 128, :] * scale2
        wt[:, s * 128 : (s + 1) * 128] = w.T.astype(BF)

    def block_at(i):
        return ahead(5 * (i + 1) % 16)

    def moment(i):
        b = block_at(i)
        part = dot_nn(wt[...], vv[:, lanes(b, 256)])
        sbuf[0] = part[:, :128]
        sbuf[1] = part[:, 128:]
        own_s[b] = sbuf[core]
        send_x[b] = sbuf[1 - core].astype(BF)
        send(send_x.at[b], recv_x.at[b], s_x, r_x.at[b], (z, mate))

    def pair_sum(i):
        b = block_at(i)
        wait(recv_x.at[b], r_x.at[b])
        return (own_s[b] + recv_x[b].astype(F32)).astype(BF), b

    def plane(i):
        value, b = pair_sum(i)
        d = 5 * (i + 1) % 16
        send_s[b] = value

        @pl.when(d // 4 > 0)
        def _():
            send(send_s.at[b, 0:HR], recv_s.at[0, cx, b % 4], s_s, r_s.at[0], (z, 2 * ((b // 4) * 4 + cy) + core))

        @pl.when(d // 4 == 0)
        def _():
            recv_s[0, cx, b % 4] = value[0:HR]

        @pl.when(d % 4 > 0)
        def _():
            send(send_s.at[b, HR:KR], recv_s.at[1, cy, b // 4], s_s, r_s.at[1], (z, 2 * (cx * 4 + b % 4) + core))

        @pl.when(d % 4 == 0)
        def _():
            recv_s[1, cy, b // 4] = value[HR:KR]

    loop(0, LAG, moment)

    def both_steps(i):
        moment(i)
        plane(i - LAG)

    loop(LAG, 16, both_steps)
    loop(16 - LAG, 16, plane)

    hot8 = jnp.concatenate([hot] * NS, axis=0)
    by_group = dot_nn(wt[...], hot8)
    groups = by_group[0:NZ]
    for r in range(1, R):
        groups = groups + by_group[r * NZ : (r + 1) * NZ]
    gw_high, gw_low = two_parts(groups)
    ev_high, ev_low = two_parts(evidence)
    for k in range(NZ):
        stage[k, R : R + 1, :] = gw_high[k : k + 1].astype(F32)
        stage[k, R + 1 : R + 2, :] = gw_low[k : k + 1].astype(F32)
        stage[k, R + 2 : R + 3, :] = jnp.broadcast_to(ev_high.astype(F32), (1, 128))
        stage[k, R + 3 : R + 4, :] = jnp.broadcast_to(ev_low.astype(F32), (1, 128))

    for half in range(2):
        wait(recv_s.at[half, pl.ds(0, 3)], r_s.at[half])
        here, source, step = (cy, cy, 1) if half == 0 else (cx, cx, 4)
        for n in range(4):
            to = (here + n) % 4
            part = recv_s[half, 0, to].astype(F32)
            for t in range(1, 4):
                part = part + recv_s[half, t, to].astype(F32)
            if n:
                send_b[half, n] = part.astype(BF)
                send(send_b.at[half, n], recv_b.at[half, source], s_b, r_b.at[half], (z, 2 * ahead(n * step) + core))
            else:
                recv_b[half, source] = part.astype(BF)
    for half in range(2):
        wait(recv_b.at[half, pl.ds(0, 3)], r_b.at[half])
        part = recv_b[half, 0].astype(F32)
        for t in range(1, 4):
            part = part + recv_b[half, t].astype(F32)
        ssum[half * HR : (half + 1) * HR, :] = part
    for k in range(NZ):
        stage[k, 0:R, :] = ssum[pl.ds(k, R, stride=NZ), :]
    send_3[...] = stage[...].astype(BF)

    def start_3(d):
        to = (z + d) % NZ
        send(send_3.at[to], recv_3.at[z], s_3, r_3, (to, g))

    for d in RING_ORDER:
        start_3(d)
    recv_3[pl.ds(z, 1)] = send_3[pl.ds(z, 1)]
    wait(recv_3.at[pl.ds(0, 15)], r_3)
    last = recv_3[0].astype(F32)
    for t in range(1, NZ):
        last = last + recv_3[t].astype(F32)
    a16[...] = last
    for row in (R, R + 2):
        high, low = two_parts(last[row : row + 1] + last[row + 1 : row + 2])
        a16[row : row + 1, :] = high.astype(F32)
        a16[row + 1 : row + 2, :] = low.astype(F32)
    fin[pl.ds(g, 1)] = a16[...].astype(BF)[None]
    tile = fin.at[g]

    def start_5(d):
        for c in range(2):
            send(tile, tile, s_5, r_5, (z, 2 * ahead(d) + c))

    for d in PLANE_ORDER:
        start_5(d)
    send(tile, tile, s_5, r_5, (z, mate))
    wait(fin.at[pl.ds(0, 31)], r_5)
    fin_out[...] = fin[...]

    wait(recv_a.at[pl.ds(0, 15)], s_a1)
    wait(a_all.at[:, pl.ds(0, 6 * 128)], s_a2)
    wait(a_all.at[0:HR, pl.ds(0, 18 * 128)], s_a2b)
    wait(a_all.at[:, pl.ds(0, HALF)], s_a3)
    wait(send_x, s_x)
    wait(recv_s.at[:, pl.ds(0, 3)], s_s)
    wait(send_b.at[:, pl.ds(0, 3)], s_b)
    wait(send_3.at[pl.ds(0, 15)], s_3)
    wait(fin.at[pl.ds(0, 31)], s_5)


def finish(fin, ctf, out, ctf_out, ev_out):
    rest = jnp.zeros((16 - R, 128), F32)
    for t in range(NC):
        for c in range(2):
            block = fin[2 * t + c].astype(F32)
            out[pl.ds(c * NC + t, R, stride=2 * NC), :] = block[0:R]
            rest = rest + block[R:16]
    groups = jnp.broadcast_to(rest[0:1] + rest[1:2], (G, 128)).T
    for t in range(HALF // 128):
        f = slice(t * 128, (t + 1) * 128)
        ctf_out[:, f] = jnp.sum(ctf[:, f] * ctf[:, f] * groups, axis=0, keepdims=True)
    ev_out[...] = (rest[2:3] + rest[3:4]) * (1.0 / (PD * NZ * NC * 2 * HALF))


def shards(dft, twiddle, particles, references, slot_class, log_prior, shift_offsets, group_ids, ctf_table, noise_power):
    vmem = pl.BlockSpec(memory_space=pltpu.VMEM)
    hbm = pl.BlockSpec(memory_space=pl.ANY)
    dma = pltpu.SemaphoreType.DMA
    tiles = pl.pallas_call(
        kernel,
        out_shape=jax.ShapeDtypeStruct((2 * NC, 16, 128), BF),
        in_specs=[hbm] * 10,
        out_specs=vmem,
        scratch_shapes=[
            pltpu.VMEM((1, R, FR), BF),
            pltpu.SMEM((NZ,), jnp.int32),
            pltpu.SMEM((NZ,), F32),
            pltpu.SMEM((2, NS), jnp.int32),
            pltpu.VMEM((1, PD), jnp.int32),
            pltpu.VMEM((1, HALF), F32),
            pltpu.VMEM((2, 8, 256), F32),
            pltpu.VMEM((PD, FR), BF),
            pltpu.VMEM((G, HALF), F32),
            pltpu.VMEM((2, 512, 512), BF),
            pltpu.VMEM((512, 512), BF),
            pltpu.VMEM((512, 512), F32),
            pltpu.VMEM((NS, HALF), F32),
            pltpu.VMEM((NS, HALF), F32),
            pltpu.VMEM((PD, HALF), F32),
            pltpu.VMEM((PD, NC * 384), BF),
            pltpu.VMEM((NS * PD, FR), BF),
            pltpu.VMEM((PD, 128), F32),
            pltpu.VMEM((KR, FR), BF),
            pltpu.VMEM((PD, KR), F32),
            pltpu.VMEM((NS * PD, KR), F32),
            pltpu.VMEM((KR, NS * PD), BF),
            pltpu.VMEM((16, 128), BF),
            pltpu.VMEM((16, 128), F32),
            pltpu.VMEM((NZ, 16, 128), BF),
            pltpu.VMEM((KR, 128), F32),
            pltpu.VMEM((2, KR, 128), F32),
            pltpu.VMEM((NC, KR, 128), F32),
            pltpu.VMEM((NC, KR, 128), BF),
            pltpu.VMEM((NC, KR, 128), BF),
            pltpu.VMEM((NC, KR, 128), BF),
            pltpu.VMEM((2, 4, 4, HR, 128), BF),
            pltpu.VMEM((2, 4, HR, 128), BF),
            pltpu.VMEM((2, 4, HR, 128), BF),
            pltpu.VMEM((KR, 128), F32),
            pltpu.VMEM((NZ, 16, 128), F32),
            pltpu.VMEM((NZ, 16, 128), BF),
            pltpu.VMEM((NZ, 16, 128), BF),
            pltpu.VMEM((2 * NC, 16, 128), BF),
            dma((10,)),
            dma, dma,
            dma, dma, dma((16,)), dma((16,)),
            dma, dma((16,)),
            dma, dma((16,)),
            dma, dma((2,)),
            dma, dma((2,)),
            dma, dma,
            dma, dma,
        ],
        compiler_params=pltpu.CompilerParams(
            collective_id=0, has_side_effects=True, vmem_limit_bytes=56 * 1024 * 1024
        ),
    )(
        particles, references, slot_class, log_prior, shift_offsets.T,
        group_ids.reshape(1, PD), ctf_table, noise_power.reshape(1, HALF), dft, twiddle,
    )
    class_sums, ctf_power, evidence = pl.pallas_call(
        finish,
        out_shape=(
            jax.ShapeDtypeStruct((R * FR // 128, 128), F32),
            jax.ShapeDtypeStruct((1, HALF), F32),
            jax.ShapeDtypeStruct((1, 128), F32),
        ),
        in_specs=[vmem, vmem],
        out_specs=(vmem, vmem, vmem),
    )(tiles, ctf_table)
    return class_sums.reshape(1, R, FR), ctf_power, evidence[0, 0]


def solution(mesh):
    dft, twiddle = dft_tables()
    split = ("gx", "gy")
    in_specs = (P(split, None), P("gx", None, None), P(), P(), P(), P(split), P(), P())
    out_specs = (P("gx", None, None), P("gx", None), P())

    def run(*args):
        body = functools.partial(shards, jnp.asarray(dft), jnp.asarray(twiddle))
        return jax.shard_map(body, mesh=mesh, in_specs=in_specs, out_specs=out_specs, check_vma=False)(*args)

    return run
```
